32 devices in a mesh: section: 2 (over core), context: 8 (over z, x), tensor: 2 (over y).
Axes of the slice: x: 2, y: 2, z: 4, core: 2. Of those that a mesh axis runs over, the one named last changes fastest.
Arguments:
- boundary: bfloat16 [2, 2, 2048, 2048], P('section', None, ('context', 'tensor')), may hold values from -6 to 6
- token_places: int32 [2, 2048], P(None, 'context'), may hold values from 0 to 2047, as said below
- lengths: int32 [2, 3], replicated, may hold values from 1 to 1024, 2048 in all within a row
- qkv_weight: bfloat16 [2, 2048, 3, 2048], P('section', 'context', None, 'tensor'), may hold values from -0.125 to 0.125
- out_weight: bfloat16 [2, 2048, 2048], P('section', 'tensor', 'context'), may hold values from -1 to 1
- fc1_weight: bfloat16 [2, 2048, 8192], P('section', 'context', 'tensor'), may hold values from -0.125 to 0.125
- fc2_weight: bfloat16 [2, 8192, 2048], P('section', 'tensor', 'context'), may hold values from -0.0625 to 0.0625
- norm_gain: float32 [2, 2, 2048], P('section'), may hold values from 0.1 to 1.9
- norm_bias: float32 [2, 2, 2048], P('section'), may hold values from -4 to 4
- qkv_bias: float32 [2, 3, 2048], P('section'), may hold values from -4 to 4
- fc1_bias: float32 [2, 8192], P('section'), may hold values from -4 to 4
- branch_bias: float32 [2, 2, 2048], P('section'), may hold values from -4 to 4
Outputs:
- boundary_result: bfloat16 [2, 2, 2048, 2048], P('section', None, ('context', 'tensor'))
- qkv_weight_grad: float32 [2, 2048, 3, 2048], P('section', 'context', None, 'tensor')
- out_weight_grad: float32 [2, 2048, 2048], P('section', 'tensor', 'context')
- fc1_weight_grad: float32 [2, 2048, 8192], P('section', 'context', 'tensor')
- fc2_weight_grad: float32 [2, 8192, 2048], P('section', 'tensor', 'context')
- norm_gain_grad: float32 [2, 2, 2048], P('section')
- norm_bias_grad: float32 [2, 2, 2048], P('section')
- qkv_bias_grad: float32 [2, 3, 2048], P('section')
- fc1_bias_grad: float32 [2, 8192], P('section')
- branch_bias_grad: float32 [2, 2, 2048], P('section')
The draws below stay inside these ranges and needn't reach their ends.
Inputs may be any that keep to these rules, and one draw needn't show every extreme that they name: `token_places`: in each micro-batch, the 256 entries of context index c are r_c, r_c + 8, r_c + 16 and so on, rising, for a permutation r of 0 to 7 drawn for each micro-batch; every packed position appears once. Each micro-batch's 3 lengths add up to 2048, and its longest is exactly 1024.
All inputs are finite; a program needn't handle non-finite values.
Results may differ from the reference program's by a relative error of at most 0.022.
Values may be sent and summed in bfloat16 or wider, within the bound.
No kernel may reach another device: no remote copies, remote signals or barrier semaphores. Data moves between devices by JAX's collectives and lax.ppermute only.
A program may use at most 384 MiB of HBM per device.

```python
import math
import jax
import jax.numpy as jnp
import numpy as np
from jax import lax

D = 2048
FF = 8192
HEADS = 8
HD = 256
ROT = 64
TOK_CTX = 256
MICRO = 2
SEQMAX = 1024
TOK_MB = 2048
NSEQ = 3
CYCLE = 8


def draw_token_places(key, part):
    key = jax.random.fold_in(key, 7)
    micro_keys = jax.random.split(key, MICRO)

    def one_micro(micro_key):
        order = jax.random.permutation(micro_key, CYCLE).astype(jnp.int32)
        row_index = jnp.arange(TOK_CTX, dtype=jnp.int32)
        return (row_index[None, :] * CYCLE + order[:, None]).reshape(CYCLE * TOK_CTX)
    return jax.vmap(one_micro)(micro_keys).astype(jnp.int32)


def block_scale(stream_key, shape, cuts, smallest, largest):
    loudness = 1.0
    for dim, parts in cuts:
        steps = jax.random.uniform(jax.random.fold_in(jax.random.fold_in(stream_key, 6), dim), (parts,), jnp.float32, smallest / len(cuts), largest / len(cuts))
        loudness = loudness * jnp.repeat(jnp.exp(steps), shape[dim] // parts).reshape((-1,) + (1,) * (len(shape) - 1 - dim))
    return loudness


def profile(count, total, bound, slope):
    loads = [(1 << 20) // math.isqrt(standing ** slope) + 1 for standing in range(2, count + 1)]
    surplus, holding = total - bound - (count - 1), [1] * (count - 1)
    while surplus > 0:
        candidates = [i for i in range(count - 1) if holding[i] < bound]
        pool, left = sum([loads[i] for i in candidates]), surplus
        for i in candidates:
            more = min(bound - holding[i], max(1, left * loads[i] // pool), surplus)
            holding[i] = holding[i] + more
            surplus = surplus - more
    return np.array([bound] + holding)


def uneven(key, count, total, limit, slope):
    if count == 2:
        one = jax.random.randint(key, (), max(1, total - limit), min(limit, total - 1) + 1)
        return jnp.stack([one, total - one])
    sizes = jnp.asarray(profile(count, total, limit, slope), jnp.int32)
    pairs = (count - 1) // 2
    giver, sink = sizes[1:1 + 2 * pairs:2], sizes[2:2 + 2 * pairs:2]
    room = jnp.minimum(giver - 1, limit - sink)
    moved = jax.random.randint(jax.random.fold_in(key, 1), (pairs,), 0, 1 << 20) % (room + 1)
    sizes = sizes.at[1:1 + 2 * pairs:2].set(giver - moved).at[2:2 + 2 * pairs:2].set(sink + moved)
    return sizes[jax.random.permutation(jax.random.fold_in(key, 2), count)]


def normal_values(stream_key, shape, deviation, limit, cuts=(), kind=jnp.bfloat16):
    factor_of = block_scale(stream_key, shape, cuts, -0.22, 0.18) if cuts else 1.0
    array = jax.random.normal(stream_key, shape, jnp.float32) * deviation * factor_of
    return jnp.minimum(jnp.maximum(array, -limit), limit).astype(kind)


def setup_inputs(seed: int = 0) -> dict:
    arg_keys = jax.random.split(jax.random.key(seed), 13)
    boundary = normal_values(arg_keys[0], (2, MICRO, TOK_MB, D), 1.0, 6.0, ((0, 2), (2, 16)))
    token_places = draw_token_places(jax.random.fold_in(arg_keys[12], 71), 0)
    lengths = jax.vmap(lambda own: uneven(own, NSEQ, TOK_MB, SEQMAX, 2))(jax.random.split(arg_keys[2], MICRO)).reshape((MICRO, NSEQ)).astype(jnp.int32)
    qkv_weight = normal_values(arg_keys[3], (2, D, 3, D), D ** -0.5, 0.125, ((0, 2), (1, 8), (3, 2)))
    out_weight = normal_values(arg_keys[4], (2, D, D), (D // 64) ** -0.5, 1.0, ((0, 2), (1, 2), (2, 8)))
    fc1_weight = normal_values(arg_keys[5], (2, D, FF), D ** -0.5, 0.125, ((0, 2), (1, 8), (2, 2)))
    fc2_weight = normal_values(arg_keys[6], (2, FF, D), FF ** -0.5, 0.0625, ((0, 2), (1, 2), (2, 8)))
    norm_gain = jnp.clip(1.0 + 0.18 * jax.random.normal(arg_keys[7], (2, 2, D), jnp.float32), 0.1, 1.9)
    norm_bias = normal_values(arg_keys[8], (2, 2, D), 0.3, 4.0, ((0, 2),), jnp.float32)
    qkv_bias = normal_values(arg_keys[9], (2, 3, D), 0.3, 4.0, ((0, 2),), jnp.float32)
    fc1_bias = normal_values(arg_keys[10], (2, FF), 0.3, 4.0, ((0, 2),), jnp.float32)
    branch_bias = normal_values(arg_keys[11], (2, 2, D), 0.3, 4.0, ((0, 2),), jnp.float32)
    return dict(boundary=boundary, token_places=token_places, lengths=lengths, qkv_weight=qkv_weight, out_weight=out_weight, fc1_weight=fc1_weight, fc2_weight=fc2_weight, norm_gain=norm_gain, norm_bias=norm_bias, qkv_bias=qkv_bias, fc1_bias=fc1_bias, branch_bias=branch_bias)


@jax.custom_vjp
def low(v):
    return lax.optimization_barrier(v.astype(jnp.bfloat16)).astype(jnp.float32)

@jax.custom_vjp
def low_back(v):
    return v

def low_keep(v):
    return (low(v), None)

def low_pass(kept, grad):
    return (grad,)

def back_keep(v):
    return (v, None)

def back_low(kept, grad):
    return (low(grad),)
low.defvjp(low_keep, low_pass)
low_back.defvjp(back_keep, back_low)
EPSILON = 1e-05
ROTARY_BASE = 10000.0
MASKED = -1e+30
HIGHEST = lax.Precision.HIGHEST

def locate(placed, lengths):
    seq_ends = jnp.cumsum(lengths).astype(jnp.int32)
    seq_starts = (seq_ends - lengths).astype(jnp.int32)
    segment = lax.optimization_barrier(jnp.sum((placed[:, None] >= seq_ends[None, :]).astype(jnp.int32), axis=1)).astype(jnp.int32)
    chosen = segment[:, None] == jnp.arange(lengths.shape[0], dtype=jnp.int32)[None, :]
    seq_begin = lax.optimization_barrier(jnp.sum(jnp.where(chosen, seq_starts[None, :], 0), axis=1)).astype(jnp.int32)
    return (segment, (placed - seq_begin).astype(jnp.int32))

def normalize(values, gain_row, bias_row):
    row_mean = lax.optimization_barrier(jnp.mean(values, axis=-1, keepdims=True))
    centered = values - row_mean
    inv_std = lax.rsqrt(lax.optimization_barrier(jnp.mean(centered * centered, axis=-1, keepdims=True)) + EPSILON)
    return centered * inv_std * gain_row + bias_row

def angles(position):
    half_rot = ROT // 2
    frequency = ROTARY_BASE ** (-(jnp.arange(half_rot, dtype=jnp.float32) * 2.0) / ROT)
    phase_angle = position.astype(jnp.float32)[:, None] * frequency[None, :]
    return (jnp.cos(phase_angle), jnp.sin(phase_angle))

def rotate_pairs(values, cosine, sine_part):
    half_rot = ROT // 2
    leading = values[..., :half_rot]
    second = values[..., half_rot:ROT]
    cos_rows = cosine[:, None, :]
    sin_rows = sine_part[:, None, :]
    return jnp.concatenate([leading * cos_rows - second * sin_rows, second * cos_rows + leading * sin_rows, values[..., ROT:]], axis=-1)

def attend(queries, key_rows, value_rows, segment, position):
    allowed = (segment[:, None] == segment[None, :]) & (position[None, :] <= position[:, None])
    score_scale = 1.0 / math.sqrt(HD)

    def one_head(pieces):
        head_query, head_key, head_value = pieces
        scores = low_back(jnp.dot(head_query, head_key.T, precision=HIGHEST) * score_scale)
        scores = jnp.where(allowed, scores, MASKED)
        row_top = lax.optimization_barrier(jnp.max(scores, axis=1, keepdims=True))
        weight = jnp.exp(scores - row_top)
        softmax_rows = weight / lax.optimization_barrier(jnp.sum(weight, axis=1, keepdims=True))
        return jnp.dot(low(softmax_rows), head_value, precision=HIGHEST)
    combined = lax.map(jax.checkpoint(one_head), (queries.transpose(1, 0, 2), key_rows.transpose(1, 0, 2), value_rows.transpose(1, 0, 2)))
    return combined.transpose(1, 0, 2)

def layer_apply(layer_input, params, layer_index, segment, position):
    qkv_w, out_w, fc1_w, fc2_w, gain_rows, bias_rows, qkv_b, fc1_b, branch_b = params
    row_count = layer_input.shape[0]
    norm_attn = low(normalize(layer_input, gain_rows[layer_index, 0], bias_rows[layer_index, 0]))
    norm_mlp = low(normalize(layer_input, gain_rows[layer_index, 1], bias_rows[layer_index, 1]))
    projected = jnp.dot(norm_attn, qkv_w[layer_index].reshape(D, 3 * D), precision=HIGHEST) + qkv_b[layer_index].reshape(3 * D)
    projected = low_back(projected).reshape(row_count, 3, HEADS, HD)
    cosine, sine_part = angles(position)
    queries = low(rotate_pairs(projected[:, 0], cosine, sine_part))
    key_rows = low(rotate_pairs(projected[:, 1], cosine, sine_part))
    value_rows = low(projected[:, 2])
    attended = attend(queries, key_rows, value_rows, segment, position).reshape(row_count, D)
    attended = low(low_back(attended))
    preact = low_back(jnp.dot(norm_mlp, fc1_w[layer_index], precision=HIGHEST) + fc1_b[layer_index])
    hidden = low(jax.nn.gelu(preact, approximate=False))
    branch = jnp.dot(attended, out_w[layer_index], precision=HIGHEST) + jnp.dot(hidden, fc2_w[layer_index], precision=HIGHEST)
    return layer_input + branch + branch_b[layer_index, 0] + branch_b[layer_index, 1]

def reference(boundary, token_places, lengths, qkv_weight, out_weight, fc1_weight, fc2_weight, norm_gain, norm_bias, qkv_bias, fc1_bias, branch_bias):
    segments, positions = jax.vmap(locate)(token_places, lengths)
    params = tuple((entry.astype(jnp.float32) for entry in (qkv_weight, out_weight, fc1_weight, fc2_weight, norm_gain, norm_bias, qkv_bias, fc1_bias, branch_bias)))
    inputs = boundary[0].astype(jnp.float32)
    cotangent = boundary[1].astype(jnp.float32)

    def run_layers(inputs, params):

        def one_micro(pieces):
            layer_input, segment, position = pieces
            middle = low(low_back(layer_apply(layer_input, params, 0, segment, position)))
            return low(layer_apply(middle, params, 1, segment, position))
        return lax.map(one_micro, (inputs, segments, positions))
    outputs, pull_back = jax.vjp(run_layers, inputs, params)
    d_inputs, d_params = pull_back(cotangent)
    result = jnp.stack([d_inputs, outputs]).astype(jnp.bfloat16)
    return (result, d_params[0], d_params[1], d_params[2], d_params[3], d_params[4], d_params[5], d_params[6], d_params[7], d_params[8])
```

```python
import math

import jax
import jax.numpy as jnp
import numpy as np
from jax import lax
from jax.sharding import PartitionSpec as P

HD = 256
ROT = 64

EPSILON = 1e-05
ROTARY_BASE = 10000.0
MASKED = -1e30

BF16 = jnp.bfloat16
F32 = jnp.float32


def locate(placed, lengths):
    seq_ends = jnp.cumsum(lengths)
    seq_starts = seq_ends - lengths
    segment = jnp.sum((placed[:, None] >= seq_ends[None, :]).astype(jnp.int32), axis=1)
    chosen = segment[:, None] == jnp.arange(lengths.shape[0], dtype=jnp.int32)[None, :]
    seq_begin = jnp.sum(jnp.where(chosen, seq_starts[None, :], 0), axis=1)
    return (segment, placed - seq_begin)


def normalize_parts(values):
    row_mean = jnp.mean(values, axis=-1, keepdims=True)
    centered = values - row_mean
    inv_std = lax.rsqrt(jnp.mean(centered * centered, axis=-1, keepdims=True) + EPSILON)
    return (centered * inv_std, inv_std)


def angles(position):
    half_rot = ROT // 2
    frequency = ROTARY_BASE ** (-(jnp.arange(half_rot, dtype=F32) * 2.0) / ROT)
    phase_angle = position.astype(F32)[:, None] * frequency[None, :]
    return (jnp.cos(phase_angle), jnp.sin(phase_angle))


def rotate_pairs(values, cosine, sine_part):
    half_rot = ROT // 2
    leading = values[:, :half_rot]
    second = values[:, half_rot:ROT]
    return jnp.concatenate(
        [
            leading * cosine - second * sine_part,
            second * cosine + leading * sine_part,
            values[:, ROT:],
        ],
        axis=-1,
    )


def gelu_exact(values):
    return jax.nn.gelu(values, approximate=False)


def dot_tn(left_side, right_side):
    return lax.dot_general(
        left_side, right_side, (((0,), (0,)), ((), ())), preferred_element_type=F32
    )


def dot_nt(left_side, right_side):
    return lax.dot_general(
        left_side, right_side, (((1,), (1,)), ((), ())), preferred_element_type=F32
    )


def dot_nn(left_side, right_side):
    return jnp.dot(left_side, right_side, preferred_element_type=F32)


def after(value, earlier):
    return lax.optimization_barrier((value, earlier))[0]


def flip(value, axis, mask):
    count = lax.axis_size(axis)
    return lax.ppermute(value, axis, [(place, place ^ mask) for place in range(count)])


def trade(value):
    return flip(value, "section", 1)


class Plan:
    def __init__(self, micro_count, heads_here, part_rows):
        self.contexts = lax.axis_size("context")
        self.tensors = lax.axis_size("tensor")
        self.micros = micro_count
        self.heads = heads_here
        self.span = self.contexts // micro_count
        self.shares = self.span // heads_here
        self.part_rows = part_rows
        self.section = lax.axis_index("section")
        self.context = lax.axis_index("context")
        self.tensor = lax.axis_index("tensor")
        self.micro = self.context // self.span
        self.share = (self.context % self.span) // heads_here
        self.head = self.context % heads_here
        self.bits = [("context", 1 << b) for b in range(int(math.log2(heads_here)))]
        self.bits += [("tensor", 1 << b) for b in range(int(math.log2(self.tensors)))]
        ways = len(self.bits)
        units = part_rows // 8
        cuts = [8 * ((units * k + ways - 1) // ways) for k in range(ways + 1)]
        self.chunks = [(cuts[k], cuts[k + 1] - cuts[k]) for k in range(ways)]
        self.orders = [self.bits[k:] + self.bits[:k] for k in range(ways)]
        head_flip, tensor_flip, row = [], [], []
        for (start, rows), order in zip(self.chunks, self.orders):
            for block in range(1 << ways):
                masks = {"context": 0, "tensor": 0}
                for place, (axis, mask) in enumerate(order):
                    if block >> place & 1:
                        masks[axis] |= mask
                head_flip += [masks["context"]] * rows
                tensor_flip += [masks["tensor"]] * rows
                row += list(range(start, start + rows))
        self.head_flip = np.array(head_flip, np.int32)
        self.tensor_flip = np.array(tensor_flip, np.int32)
        self.row = np.array(row, np.int32)
        self.rows = len(row)

    def cut(self, own):
        return [own[start : start + rows] for start, rows in self.chunks]

    def spread(self, own):
        held = self.cut(own)
        for step in range(len(self.bits)):
            came = [flip(v, *order[step]) for v, order in zip(held, self.orders)]
            held = [jnp.concatenate([v, w], axis=0) for v, w in zip(held, came)]
        return held

    def collect_chunk(self, which, value):
        value = value.astype(BF16)
        for bit in reversed(self.orders[which]):
            half = value.shape[0] // 2
            came = flip(value[half:], *bit)
            total = value[:half].astype(F32) + came.astype(F32)
            value = total.astype(BF16)
        return total

    def rows_of(self, places, section, share):
        context = section * self.span + share * self.heads + (self.head ^ self.head_flip)
        chosen = context[:, None] == jnp.arange(self.contexts, dtype=jnp.int32)[None, :]
        first = jnp.sum(jnp.where(chosen, places[None, :], 0), axis=1)
        within = (self.tensor ^ self.tensor_flip) * self.part_rows + self.row
        return first + within * self.contexts


def per_device(
    boundary,
    token_places,
    lengths,
    qkv_weight,
    out_weight,
    fc1_weight,
    fc2_weight,
    norm_gain,
    norm_bias,
    qkv_bias,
    fc1_bias,
    branch_bias,
):
    micro_count, part_rows, width = boundary.shape[1:]
    depth = qkv_weight.shape[1]
    heads_here = qkv_weight.shape[3] // HD
    units = fc1_weight.shape[2] // heads_here
    plan = Plan(micro_count, heads_here, part_rows)
    section, span, contexts = plan.section, plan.span, plan.contexts
    half_head, half_units = HD // 2, units // 2
    copies = micro_count * plan.shares
    score_scale = 1.0 / math.sqrt(HD)

    def flat(place_section, place_context):
        return place_section * contexts + place_context

    def bring(origin):
        came = []
        for micro in range(micro_count):
            pairs = [
                (flat(origin, side * span + k), flat(side, micro * span + k))
                for side in range(micro_count)
                for k in range(span)
            ]
            came.append(lax.ppermute(boundary[0, micro], ("section", "context"), pairs))
        return jnp.where(plan.micro == 0, came[0], came[1])

    def take_home(own, target):
        came = []
        for micro in range(micro_count):
            pairs = [
                (flat(side, micro * span + k), flat(target, side * span + k))
                for side in range(micro_count)
                for k in range(span)
            ]
            came.append(lax.ppermute(own, ("section", "context"), pairs))
        return jnp.stack(came)

    first_places = lax.all_gather(token_places[:, 0], "context", axis=0)
    places = lax.dynamic_index_in_dim(first_places, plan.micro, 1, keepdims=False)
    own_lengths = lax.dynamic_index_in_dim(lengths, plan.micro, 0, keepdims=False)
    segment, position = locate(plan.rows_of(places, section, plan.share), own_lengths)
    key_spots = [
        locate(plan.rows_of(places, section ^ side, plan.share ^ share), own_lengths)
        for side in range(2)
        for share in range(plan.shares)
    ]
    seg_keys = jnp.concatenate([spot[0] for spot in key_spots])
    pos_keys = jnp.concatenate([spot[1] for spot in key_spots])
    allowed = (segment[:, None] == seg_keys[None, :]) & (pos_keys[None, :] <= position[:, None])
    cosine, sine_part = angles(position)

    def share_keys(value):
        held = [value]
        for share in range(1, plan.shares):
            held.append(flip(value, "context", share * heads_here))
        pile = jnp.concatenate(held, axis=0)
        return jnp.concatenate([pile, trade(pile)], axis=0)

    def return_keys(value):
        half = value.shape[0] // 2
        pile = value[:half] + trade(value[half:].astype(BF16)).astype(F32)
        total = pile[: plan.rows]
        for share in range(1, plan.shares):
            piece = pile[share * plan.rows : (share + 1) * plan.rows].astype(BF16)
            total = total + flip(piece, "context", share * heads_here).astype(F32)
        return total

    def both_layers(halves):
        kept = lax.dynamic_index_in_dim(halves, section, 0, keepdims=False)
        sent = lax.dynamic_index_in_dim(halves, 1 - section, 0, keepdims=False)
        came = trade(sent)
        return [jnp.where(section == layer, kept, came) for layer in range(2)]

    def deal(blocks):
        spread = jnp.broadcast_to(blocks[None], (copies,) + blocks.shape)
        spread = spread.reshape((contexts,) + blocks.shape[1:])
        return lax.all_to_all(spread, "context", split_axis=0, concat_axis=0, tiled=True)

    qkv_halves = both_layers(
        qkv_weight[0]
        .reshape(depth, 3, heads_here, 2, half_head)
        .transpose(3, 2, 0, 1, 4)
        .reshape(2, heads_here, depth, 3 * half_head)
    )
    fc1_halves = both_layers(
        fc1_weight[0].reshape(depth, heads_here, 2, half_units).transpose(2, 1, 0, 3)
    )
    push_halves = both_layers(
        jnp.concatenate(
            [
                out_weight[0].reshape(heads_here, 2, half_head, depth),
                fc2_weight[0].reshape(heads_here, 2, half_units, depth),
            ],
            axis=2,
        ).transpose(1, 0, 2, 3)
    )

    def in_order(own, other):
        return (jnp.where(section == 0, own, other), jnp.where(section == 0, other, own))

    def gather_layer(layer, earlier):
        blocks = qkv_halves[layer]
        if earlier is not None:
            blocks = after(blocks, earlier)
        qkv_dealt = deal(blocks)
        fc1_dealt = deal(after(fc1_halves[layer], qkv_dealt))
        push_dealt = deal(after(push_halves[layer], fc1_dealt))
        qkv_own = qkv_dealt.reshape(width, 3, half_head)
        low, high = in_order(qkv_own, trade(qkv_own))
        qkv_full = jnp.stack([low, high], axis=2).reshape(width, 3 * HD)
        fc1_own = fc1_dealt.reshape(width, half_units)
        fc1_full = jnp.concatenate([fc1_own, trade(fc1_own)], axis=1)
        push_own = push_dealt.transpose(1, 0, 2).reshape(half_head + half_units, width)
        push_full = jnp.concatenate([push_own, trade(push_own)], axis=0)
        return (qkv_full, fc1_full, push_full), push_dealt

    head_index = plan.tensor * heads_here + plan.head
    both_gain = jnp.where(section == 0, norm_gain[0], trade(norm_gain[0]))
    both_gain = [both_gain, jnp.where(section == 1, norm_gain[0], trade(norm_gain[0]))]
    both_bias = [jnp.where(section == l, norm_bias[0], trade(norm_bias[0])) for l in range(2)]
    qkv_shift_own = lax.dynamic_slice(qkv_bias[0], (0, head_index * HD), (3, HD)).reshape(3 * HD)
    unit_shift_own = lax.dynamic_slice_in_dim(fc1_bias[0], head_index * units, units)
    out_shift_own = branch_bias[0, 0] + branch_bias[0, 1]
    qkv_shift = [jnp.where(section == l, qkv_shift_own, trade(qkv_shift_own)) for l in range(2)]
    unit_shift = [jnp.where(section == l, unit_shift_own, trade(unit_shift_own)) for l in range(2)]
    out_shift = [jnp.where(section == l, out_shift_own, trade(out_shift_own)) for l in range(2)]

    def unit_order(values):
        low, high = values[..., :half_units], values[..., half_units:]
        first, second = in_order(low, high)
        return jnp.concatenate([first, second], axis=-1)

    unit_shift = [unit_order(shift) for shift in unit_shift]

    def forward(layer, own_rows, weights):
        qkv_full, fc1_full, push_full = weights
        full_rows = jnp.concatenate(plan.spread(own_rows), axis=0)
        scaled, _ = normalize_parts(full_rows.astype(F32))
        norm_attn = (scaled * both_gain[layer][0] + both_bias[layer][0]).astype(BF16)
        norm_mlp = (scaled * both_gain[layer][1] + both_bias[layer][1]).astype(BF16)
        projected = dot_nn(norm_attn, qkv_full) + qkv_shift[layer]
        queries = rotate_pairs(projected[:, :HD], cosine, sine_part).astype(BF16)
        key_rows = rotate_pairs(projected[:, HD : 2 * HD], cosine, sine_part).astype(BF16)
        value_rows = projected[:, 2 * HD :].astype(BF16)
        key_value = share_keys(jnp.concatenate([key_rows, value_rows], axis=1))
        keys, values = key_value[:, :HD], key_value[:, HD:]
        scores = dot_nt(queries, keys) * score_scale
        masked = jnp.where(allowed, scores, MASKED)
        top = jnp.max(masked, axis=1, keepdims=True)
        weight = jnp.where(allowed, jnp.exp(masked - top), 0.0)
        denominator = jnp.sum(weight, axis=1, keepdims=True)
        attended = (dot_nn(weight.astype(BF16), values) / denominator).astype(BF16)
        log_total = top + jnp.log(denominator)
        preact = dot_nn(norm_mlp, fc1_full) + unit_shift[layer]
        hidden = gelu_exact(preact).astype(BF16)
        first, second = in_order(attended[:, :half_head], attended[:, half_head:])
        pushed = jnp.concatenate(
            [first, hidden[:, :half_units], second, hidden[:, half_units:]], axis=1
        )
        sums = []
        start = 0
        for which, (_, rows) in enumerate(plan.chunks):
            count = rows << len(plan.bits)
            part = dot_nn(pushed[start : start + count], push_full).astype(BF16)
            sums.append(plan.collect_chunk(which, part))
            start += count
        summed = jnp.concatenate(sums, axis=0)
        output = (own_rows.astype(F32) + summed + out_shift[layer]).astype(BF16)
        kept = (full_rows, norm_attn, norm_mlp, queries, keys, values, log_total, preact, pushed)
        return output, kept

    def backward(layer, grad_own, grad_full, own_rows, kept, weights):
        qkv_full, fc1_full, push_full = weights
        full_rows, norm_attn, norm_mlp, queries, keys, values, log_total, preact, pushed = kept
        d_pushed = dot_nt(grad_full, push_full)
        push_grad = dot_tn(pushed, grad_full)
        cut = half_head + half_units
        first, second = in_order(d_pushed[:, :half_head], d_pushed[:, cut : cut + half_head])
        d_attended = jnp.concatenate([first, second], axis=1).astype(BF16)
        d_hidden = jnp.concatenate(
            [d_pushed[:, half_head:cut], d_pushed[:, cut + half_head :]], axis=1
        )
        _, gelu_pull = jax.vjp(gelu_exact, preact)
        d_preact = gelu_pull(d_hidden)[0].astype(BF16)
        fc1_grad = dot_tn(norm_mlp, d_preact)
        scores = dot_nt(queries, keys) * score_scale
        probs = jnp.where(allowed, jnp.exp(scores - log_total), 0.0)
        d_probs = dot_nt(d_attended, values)
        centre = jnp.sum(probs * d_probs, axis=1, keepdims=True)
        d_scores = (probs * (d_probs - centre)).astype(BF16)
        d_queries = dot_nn(d_scores, keys) * score_scale
        d_keys = dot_tn(d_scores, queries) * score_scale
        d_values = dot_tn(probs.astype(BF16), d_attended)
        key_grads = return_keys(jnp.concatenate([d_keys, d_values], axis=1))
        d_projected = jnp.concatenate(
            [
                rotate_pairs(d_queries, cosine, -sine_part),
                rotate_pairs(key_grads[:, :HD], cosine, -sine_part),
                key_grads[:, HD:],
            ],
            axis=1,
        ).astype(BF16)
        qkv_grad = dot_tn(norm_attn, d_projected)
        scaled, _ = normalize_parts(full_rows.astype(F32))
        gain = both_gain[layer]
        d_norm_attn = dot_nt(d_projected, qkv_full)
        d_norm_mlp = dot_nt(d_preact, fc1_full)
        d_scaled_part = (d_norm_attn * gain[0] + d_norm_mlp * gain[1]).astype(BF16)
        sums = []
        start = 0
        for which, (_, rows) in enumerate(plan.chunks):
            count = rows << len(plan.bits)
            sums.append(plan.collect_chunk(which, d_scaled_part[start : start + count]))
            start += count
        d_scaled = jnp.concatenate(sums, axis=0)
        own_scaled, own_inv = normalize_parts(own_rows.astype(F32))
        wide = grad_own.astype(F32)
        d_input = wide + own_inv * (
            d_scaled
            - jnp.mean(d_scaled, axis=-1, keepdims=True)
            - own_scaled * jnp.mean(d_scaled * own_scaled, axis=-1, keepdims=True)
        )
        unit_sum = unit_order(jnp.sum(d_preact, axis=0, dtype=F32))
        vectors = (
            jnp.stack([jnp.sum(d_norm_attn * scaled, axis=0), jnp.sum(d_norm_mlp * scaled, axis=0)]),
            jnp.stack([jnp.sum(d_norm_attn, axis=0), jnp.sum(d_norm_mlp, axis=0)]),
            lax.dynamic_update_slice(
                jnp.zeros((3, width), F32),
                jnp.sum(d_projected, axis=0, dtype=F32).reshape(3, HD),
                (0, head_index * HD),
            ),
            lax.dynamic_update_slice_in_dim(
                jnp.zeros((fc1_bias.shape[1],), F32), unit_sum, head_index * units, 0
            ),
            jnp.sum(wide, axis=0),
        )
        return d_input.astype(BF16), vectors, (qkv_grad, fc1_grad, push_grad)

    def return_layer(grads):
        qkv_grad, fc1_grad, push_grad = grads

        def halve(value, axis, relative):
            low = lax.index_in_dim(value, 0, axis, keepdims=False)
            high = lax.index_in_dim(value, 1, axis, keepdims=False)
            own, other = (low, high) if relative else in_order(low, high)
            return (own + trade(other.astype(BF16)).astype(F32)).astype(BF16)

        def undeal(value):
            came = lax.all_to_all(value, "context", split_axis=0, concat_axis=0, tiled=True)
            came = came.reshape((copies, heads_here) + value.shape[1:])
            return jnp.sum(came.astype(F32), axis=0)

        push_half = halve(push_grad.reshape(2, half_head + half_units, width), 0, True)
        push_sum = undeal(
            push_half.reshape(half_head + half_units, contexts, depth).transpose(1, 0, 2)
        )
        fc1_half = halve(fc1_grad.reshape(width, 2, half_units), 1, True)
        fc1_sum = undeal(fc1_half.reshape(contexts, depth, half_units))
        qkv_half = halve(qkv_grad.reshape(width, 3, 2, half_head), 2, False)
        qkv_sum = undeal(qkv_half.reshape(contexts, depth, 3 * half_head))
        return qkv_sum, fc1_sum, push_sum

    first_rows = bring(0)
    weights0, done0 = gather_layer(0, None)
    weights1, _ = gather_layer(1, done0)
    middle_rows, kept0 = forward(0, first_rows, weights0)
    grad1 = after(bring(1), done0)
    grad1_full = jnp.concatenate(plan.spread(grad1), axis=0)
    last_rows, kept1 = forward(1, middle_rows, weights1)
    grad0, vectors1, grads1 = backward(1, grad1, grad1_full, middle_rows, kept1, weights1)
    sums1 = return_layer(grads1)
    grad0_full = jnp.concatenate(plan.spread(grad0), axis=0)
    d_input, vectors0, grads0 = backward(0, grad0, grad0_full, first_rows, kept0, weights0)
    sums0 = return_layer(grads0)

    result = jnp.where(section == 0, take_home(d_input, 0), take_home(last_rows, 1))
    everywhere = ("section", "context", "tensor")
    vectors1 = lax.psum(vectors1, everywhere)
    vectors0 = lax.psum(vectors0, everywhere)
    gain_sum, shift_sum, qkv_bias_sum, unit_bias_sum, branch_sum = jax.tree.map(
        lambda zero, one: jnp.where(section == 0, zero, one), vectors0, vectors1
    )

    def finish(sum0, sum1):
        mine = jnp.where(section == 0, sum0, sum1)
        yours = jnp.where(section == 0, sum1, sum0)
        low, high = in_order(mine, trade(yours.astype(BF16)).astype(F32))
        return jnp.stack([low, high])

    qkv_all, fc1_all, push_all = [finish(a, b) for a, b in zip(sums0, sums1)]
    qkv_out = (
        qkv_all.reshape(2, heads_here, depth, 3, half_head)
        .transpose(2, 3, 1, 0, 4)
        .reshape(depth, 3, heads_here * HD)
    )
    fc1_out = fc1_all.transpose(2, 1, 0, 3).reshape(depth, heads_here * units)
    out_out = push_all[:, :, :half_head].transpose(1, 0, 2, 3).reshape(heads_here * HD, depth)
    fc2_out = push_all[:, :, half_head:].transpose(1, 0, 2, 3).reshape(heads_here * units, depth)
    return (
        result[None],
        qkv_out[None],
        out_out[None],
        fc1_out[None],
        fc2_out[None],
        gain_sum[None],
        shift_sum[None],
        qkv_bias_sum[None],
        unit_bias_sum[None],
        jnp.broadcast_to(branch_sum, (2, width))[None],
    )


def solution(mesh):
    return jax.shard_map(
        per_device,
        mesh=mesh,
        in_specs=(
            P("section", None, ("context", "tensor"), None),
            P(None, "context"),
            P(),
            P("section", "context", None, "tensor"),
            P("section", "tensor", "context"),
            P("section", "context", "tensor"),
            P("section", "tensor", "context"),
            P("section", None, None),
            P("section", None, None),
            P("section", None, None),
            P("section", None),
            P("section", None, None),
        ),
        out_specs=(
            P("section", None, ("context", "tensor"), None),
            P("section", "context", None, "tensor"),
            P("section", "tensor", "context"),
            P("section", "context", "tensor"),
            P("section", "tensor", "context"),
            P("section", None, None),
            P("section", None, None),
            P("section", None, None),
            P("section", None),
            P("section", None, None),
        ),
        check_vma=False,
    )
```

```python
import math

import jax
import jax.numpy as jnp
import numpy as np
from jax import lax
from jax.sharding import PartitionSpec as P

HD = 256
ROT = 64

EPSILON = 1e-05
ROTARY_BASE = 10000.0
MASKED = -1e30

BF16 = jnp.bfloat16
F32 = jnp.float32


def locate(placed, lengths):
    seq_ends = jnp.cumsum(lengths)
    seq_starts = seq_ends - lengths
    segment = jnp.sum((placed[:, None] >= seq_ends[None, :]).astype(jnp.int32), axis=1)
    chosen = segment[:, None] == jnp.arange(lengths.shape[0], dtype=jnp.int32)[None, :]
    seq_begin = jnp.sum(jnp.where(chosen, seq_starts[None, :], 0), axis=1)
    return (segment, placed - seq_begin)


def normalize_parts(values):
    row_mean = jnp.mean(values, axis=-1, keepdims=True)
    centered = values - row_mean
    inv_std = lax.rsqrt(jnp.mean(centered * centered, axis=-1, keepdims=True) + EPSILON)
    return (centered * inv_std, inv_std)


def angles(position):
    half_rot = ROT // 2
    frequency = ROTARY_BASE ** (-(jnp.arange(half_rot, dtype=F32) * 2.0) / ROT)
    phase_angle = position.astype(F32)[:, None] * frequency[None, :]
    return (jnp.cos(phase_angle), jnp.sin(phase_angle))


def rotate_pairs(values, cosine, sine_part):
    half_rot = ROT // 2
    leading = values[:, :half_rot]
    second = values[:, half_rot:ROT]
    return jnp.concatenate(
        [
            leading * cosine - second * sine_part,
            second * cosine + leading * sine_part,
            values[:, ROT:],
        ],
        axis=-1,
    )


def dot_tn(left_side, right_side):
    return lax.dot_general(
        left_side, right_side, (((0,), (0,)), ((), ())), preferred_element_type=F32
    )


def dot_nt(left_side, right_side):
    return lax.dot_general(
        left_side, right_side, (((1,), (1,)), ((), ())), preferred_element_type=F32
    )


def dot_nn(left_side, right_side):
    return jnp.dot(left_side, right_side, preferred_element_type=F32)


def pin(*values):
    return lax.optimization_barrier(values)


def flip(value, axis, mask):
    count = lax.axis_size(axis)
    return lax.ppermute(value, axis, [(place, place ^ mask) for place in range(count)])


def trade(value):
    return flip(value, "section", 1)


class Plan:
    def __init__(self, micro_count, heads_here, part_rows):
        self.contexts = lax.axis_size("context")
        self.tensors = lax.axis_size("tensor")
        self.heads = heads_here
        self.span = self.contexts // micro_count
        self.shares = self.span // heads_here
        self.part_rows = part_rows
        self.section = lax.axis_index("section")
        self.context = lax.axis_index("context")
        self.tensor = lax.axis_index("tensor")
        self.micro = self.context // self.span
        self.share = (self.context % self.span) // heads_here
        self.head = self.context % heads_here
        bits = [("context", 1 << b) for b in range(int(math.log2(heads_here)))]
        bits += [("tensor", 1 << b) for b in range(int(math.log2(self.tensors)))]
        ways = len(bits)
        cuts = [8 * ((part_rows // 8 * k + ways - 1) // ways) for k in range(ways + 1)]
        self.chunks = [(cuts[k], cuts[k + 1] - cuts[k]) for k in range(ways)]
        self.orders = [bits[k:] + bits[:k] for k in range(ways)]
        self.partners = 1 << ways
        head_flip, tensor_flip, row = [], [], []
        for (start, rows), order in zip(self.chunks, self.orders):
            for block in range(self.partners):
                masks = {"context": 0, "tensor": 0}
                for place, (axis, mask) in enumerate(order):
                    if block >> place & 1:
                        masks[axis] |= mask
                head_flip += [masks["context"]] * rows
                tensor_flip += [masks["tensor"]] * rows
                row += list(range(start, start + rows))
        self.head_flip = np.array(head_flip, np.int32)
        self.tensor_flip = np.array(tensor_flip, np.int32)
        self.row = np.array(row, np.int32)
        self.rows = len(row)

    def cut(self, full):
        return [
            full[start * self.partners : (start + rows) * self.partners]
            for start, rows in self.chunks
        ]

    def spread(self, own, pins=()):
        held = [own[start : start + rows] for start, rows in self.chunks]
        steps = len(self.chunks)
        for step in range(steps):
            if step < len(pins) and pins[step] is not None:
                held = pins[step](held)
            came = [flip(v, *order[step]) for v, order in zip(held, self.orders)]
            if step < steps - 1:
                held = [jnp.concatenate([v, w], axis=0) for v, w in zip(held, came)]
        return jnp.concatenate([v for pair in zip(held, came) for v in pair], axis=0)

    def collect(self, parts, pin=None):
        held = [part.astype(BF16) for part in parts]
        for step in reversed(range(len(self.chunks))):
            if pin is not None and step == 0:
                held = pin(held)
            came = [
                flip(v[v.shape[0] // 2 :], *order[step]) for v, order in zip(held, self.orders)
            ]
            total = [
                v[: v.shape[0] // 2].astype(F32) + w.astype(F32) for v, w in zip(held, came)
            ]
            held = [v.astype(BF16) for v in total]
        return jnp.concatenate(total, axis=0)

    def rows_of(self, places, section, share):
        context = section * self.span + share * self.heads + (self.head ^ self.head_flip)
        apart = context ^ self.context
        chosen = apart[:, None] == jnp.arange(self.contexts, dtype=jnp.int32)[None, :]
        first = jnp.sum(jnp.where(chosen, places[None, :], 0), axis=1)
        within = (self.tensor ^ self.tensor_flip) * self.part_rows + self.row
        return first + within * self.contexts


def per_device(
    boundary,
    token_places,
    lengths,
    qkv_weight,
    out_weight,
    fc1_weight,
    fc2_weight,
    norm_gain,
    norm_bias,
    qkv_bias,
    fc1_bias,
    branch_bias,
):
    micro_count, part_rows, width = boundary.shape[1:]
    depth = qkv_weight.shape[1]
    heads_here = qkv_weight.shape[3] // HD
    units = fc1_weight.shape[2] // heads_here
    all_units = fc1_bias.shape[1]
    plan = Plan(micro_count, heads_here, part_rows)
    section, span, contexts = plan.section, plan.span, plan.contexts
    half_head, half_units = HD // 2, units // 2
    half_push = half_head + half_units
    copies = micro_count * plan.shares
    score_scale = 1.0 / math.sqrt(HD)
    head_index = plan.tensor * heads_here + plan.head

    def in_order(own, other):
        return (jnp.where(section == 0, own, other), jnp.where(section == 0, other, own))

    def flat(place_section, place_context):
        return place_section * contexts + place_context

    def bring(origin, held):
        came = []
        for micro in range(micro_count):
            pairs = [
                (flat(origin, side * span + k), flat(side, micro * span + k))
                for side in range(micro_count)
                for k in range(span)
            ]
            came.append(lax.ppermute(held[micro], ("section", "context"), pairs))
        return jnp.where(plan.micro == 0, came[0], came[1])

    def take_home(own, target):
        came = []
        for micro in range(micro_count):
            pairs = [
                (flat(side, micro * span + k), flat(target, side * span + k))
                for side in range(micro_count)
                for k in range(span)
            ]
            came.append(lax.ppermute(own, ("section", "context"), pairs))
        return jnp.stack(came)

    def half_of(halves):
        kept = lax.dynamic_index_in_dim(halves, section, 0, keepdims=False)
        came = trade(lax.dynamic_index_in_dim(halves, 1 - section, 0, keepdims=False))
        return in_order(kept, came)

    def exchange(blocks):
        return lax.all_to_all(blocks, "context", split_axis=0, concat_axis=0, tiled=True)

    def repeat(blocks):
        spread = jnp.broadcast_to(blocks[None], (copies,) + blocks.shape)
        return spread.reshape((contexts,) + blocks.shape[1:])

    def split_qkv():
        blocks = qkv_weight[0].reshape(depth, 3, heads_here, 2, half_head)
        return half_of(blocks.transpose(3, 2, 0, 1, 4).reshape(2, heads_here, depth, 3 * half_head))

    def split_fc1():
        blocks = fc1_weight[0].reshape(depth, heads_here, 2, half_units)
        return half_of(blocks.transpose(2, 1, 0, 3))

    def split_push():
        blocks = jnp.concatenate(
            [
                out_weight[0].reshape(heads_here, 2, half_head, depth),
                fc2_weight[0].reshape(heads_here, 2, half_units, depth),
            ],
            axis=2,
        )
        return half_of(blocks.transpose(1, 0, 2, 3))

    def join_qkv(dealt):
        own = dealt.reshape(width, 3, half_head)
        low, high = in_order(own, trade(own))
        return jnp.stack([low, high], axis=2).reshape(width, 3 * HD)

    def join_fc1(dealt):
        own = dealt.reshape(width, half_units)
        return jnp.concatenate([own, trade(own)], axis=1)

    def join_push(dealt):
        own = dealt.transpose(1, 0, 2).reshape(half_push, width)
        return jnp.concatenate([own, trade(own)], axis=0)

    def find_places():
        first = token_places[:, 0]
        held = lax.dynamic_index_in_dim(first, plan.micro, 0, keepdims=True)
        other = lax.dynamic_index_in_dim(first, 1 - plan.micro, 0, keepdims=True)
        pair = jnp.stack([held, other], axis=1)
        for bit in range(int(math.log2(contexts))):
            came = flip(pair, "context", 1 << bit)
            if 1 << bit >= span:
                came = came[:, ::-1]
            pair = jnp.concatenate([pair, came], axis=0)
        places = pair[:, 0]
        own_lengths = lax.dynamic_index_in_dim(lengths, plan.micro, 0, keepdims=False)
        own_spot = locate(plan.rows_of(places, section, plan.share), own_lengths)
        key_spots = [
            locate(plan.rows_of(places, section ^ side, plan.share ^ share), own_lengths)
            for side in range(2)
            for share in range(plan.shares)
        ]
        return own_spot, [jnp.concatenate(part) for part in zip(*key_spots)]

    def share_keys(value):
        held = [value]
        for share in range(1, plan.shares):
            held.append(flip(value, "context", share * heads_here))
        pile = jnp.concatenate(held, axis=0)
        return jnp.concatenate([pile, trade(pile)], axis=0)

    def return_keys(value):
        half = value.shape[0] // 2
        pile = value[:half] + trade(value[half:].astype(BF16)).astype(F32)
        total = pile[: plan.rows]
        for share in range(1, plan.shares):
            piece = pile[share * plan.rows : (share + 1) * plan.rows].astype(BF16)
            total = total + flip(piece, "context", share * heads_here).astype(F32)
        return total

    own_vector = jnp.concatenate(
        [
            norm_gain[0].reshape(-1),
            norm_bias[0].reshape(-1),
            branch_bias[0, 0] + branch_bias[0, 1],
            lax.dynamic_slice(qkv_bias[0], (0, head_index * HD), (3, HD)).reshape(-1),
            lax.dynamic_slice_in_dim(fc1_bias[0], head_index * units, units),
        ]
    )

    def unit_order(values):
        first, second = in_order(values[..., :half_units], values[..., half_units:])
        return jnp.concatenate([first, second], axis=-1)

    def cut_vector(vector):
        gain = vector[: 2 * width].reshape(2, width)
        bias = vector[2 * width : 4 * width].reshape(2, width)
        out_shift = vector[4 * width : 5 * width]
        qkv_shift = vector[5 * width : 5 * width + 3 * HD]
        return gain, bias, out_shift, qkv_shift, unit_order(vector[5 * width + 3 * HD :])

    def scaled_rows(full_rows):
        return normalize_parts(full_rows.astype(F32))[0]

    def norms(full_rows, vectors):
        gain, bias = vectors[:2]
        scaled = scaled_rows(full_rows)
        return [(scaled * gain[k] + bias[k]).astype(BF16) for k in range(2)]

    def project(norm_attn, qkv_full, vectors):
        projected = dot_nn(norm_attn, qkv_full) + vectors[3]
        queries = rotate_pairs(projected[:, :HD], cosine, sine_part).astype(BF16)
        key_rows = rotate_pairs(projected[:, HD : 2 * HD], cosine, sine_part).astype(BF16)
        value_rows = projected[:, 2 * HD :].astype(BF16)
        key_value = share_keys(jnp.concatenate([key_rows, value_rows], axis=1))
        return queries, key_value[:, :HD], key_value[:, HD:]

    def attend(queries, keys, values):
        scores = dot_nt(queries, keys) * score_scale
        masked = jnp.where(allowed, scores, MASKED)
        top = jnp.max(masked, axis=1, keepdims=True)
        weight = jnp.where(allowed, jnp.exp(masked - top), 0.0)
        denominator = jnp.sum(weight, axis=1, keepdims=True)
        attended = (dot_nn(weight.astype(BF16), values) / denominator).astype(BF16)
        return attended, top + jnp.log(denominator)

    def attend_back(queries, keys, values, log_total, d_attended):
        scores = dot_nt(queries, keys) * score_scale
        probs = jnp.where(allowed, jnp.exp(scores - log_total), 0.0)
        d_probs = dot_nt(d_attended, values)
        centre = jnp.sum(probs * d_probs, axis=1, keepdims=True)
        d_scores = (probs * (d_probs - centre)).astype(BF16)
        d_queries = dot_nn(d_scores, keys) * score_scale
        d_keys = dot_tn(d_scores, queries) * score_scale
        d_values = dot_tn(probs.astype(BF16), d_attended)
        key_grads = return_keys(jnp.concatenate([d_keys, d_values], axis=1))
        return jnp.concatenate(
            [
                rotate_pairs(d_queries, cosine, -sine_part),
                rotate_pairs(key_grads[:, :HD], cosine, -sine_part),
                key_grads[:, HD:],
            ],
            axis=1,
        ).astype(BF16)

    def join_pushed(attended, hidden):
        first, second = in_order(attended[:, :half_head], attended[:, half_head:])
        return jnp.concatenate(
            [first, hidden[:, :half_units], second, hidden[:, half_units:]], axis=1
        )

    def cut_pushed(d_pushed):
        first, second = in_order(
            d_pushed[:, :half_head], d_pushed[:, half_push : half_push + half_head]
        )
        d_attended = jnp.concatenate([first, second], axis=1).astype(BF16)
        d_hidden = jnp.concatenate(
            [d_pushed[:, half_head:half_push], d_pushed[:, half_push + half_head :]], axis=1
        )
        return d_attended, d_hidden

    def push(pushed, push_full):
        return [dot_nn(rows, push_full).astype(BF16) for rows in plan.cut(pushed)]

    def add_branch(own_rows, summed, vectors):
        return (own_rows.astype(F32) + summed + vectors[2]).astype(BF16)

    def sum_cores(rows, own, other):
        came = trade(dot_tn(rows, other).astype(BF16))
        return (dot_tn(rows, own) + came.astype(F32)).astype(BF16)

    def push_blocks(pushed, grad_full):
        came = trade(dot_tn(pushed[:, half_push:], grad_full).astype(BF16))
        half = (dot_tn(pushed[:, :half_push], grad_full) + came.astype(F32)).astype(BF16)
        return half.reshape(half_push, contexts, depth).transpose(1, 0, 2)

    def fc1_blocks(norm_mlp, d_preact):
        half = sum_cores(norm_mlp, d_preact[:, :half_units], d_preact[:, half_units:])
        return half.reshape(contexts, depth, half_units)

    def qkv_blocks(norm_attn, d_projected):
        parts = d_projected.reshape(plan.rows, 3, 2, half_head)
        own, other = in_order(parts[:, :, 0], parts[:, :, 1])
        shape = (plan.rows, 3 * half_head)
        half = sum_cores(norm_attn, own.reshape(shape), other.reshape(shape))
        return half.reshape(contexts, depth, 3 * half_head)

    def gather_sum(came):
        return jnp.sum(came.reshape((copies, heads_here) + came.shape[1:]).astype(F32), axis=0)

    def norm_grads(d_projected, d_preact, qkv_full, fc1_full, full_rows, vectors):
        d_norm_attn = dot_nt(d_projected, qkv_full)
        d_norm_mlp = dot_nt(d_preact, fc1_full)
        gain = vectors[0]
        d_scaled = (d_norm_attn * gain[0] + d_norm_mlp * gain[1]).astype(BF16)
        scaled = scaled_rows(full_rows)
        sums = [
            jnp.sum(d_norm_attn * scaled, axis=0),
            jnp.sum(d_norm_mlp * scaled, axis=0),
            jnp.sum(d_norm_attn, axis=0),
            jnp.sum(d_norm_mlp, axis=0),
        ]
        return d_scaled, sums

    def input_grad(grad_own, own_rows, d_scaled):
        own_scaled, own_inv = normalize_parts(own_rows.astype(F32))
        d_input = grad_own.astype(F32) + own_inv * (
            d_scaled
            - jnp.mean(d_scaled, axis=-1, keepdims=True)
            - own_scaled * jnp.mean(d_scaled * own_scaled, axis=-1, keepdims=True)
        )
        return d_input.astype(BF16)

    def vector_sums(norm_sums, d_projected, d_preact, grad_own):
        qkv_part = lax.dynamic_update_slice(
            jnp.zeros((3, width), F32),
            jnp.sum(d_projected, axis=0, dtype=F32).reshape(3, HD),
            (0, head_index * HD),
        )
        unit_part = lax.dynamic_update_slice_in_dim(
            jnp.zeros((all_units,), F32),
            unit_order(jnp.sum(d_preact, axis=0, dtype=F32)),
            head_index * units,
            0,
        )
        return jnp.concatenate(
            norm_sums
            + [jnp.sum(grad_own.astype(F32), axis=0), qkv_part.reshape(-1), unit_part]
        )

    def sum_everywhere(total):
        for axis in ("section", "tensor", "context"):
            for bit in range(int(math.log2(lax.axis_size(axis)))):
                total = total + flip(total, axis, 1 << bit)
        return total

    def open_units(norm_mlp, fc1_full, vectors):
        preact = dot_nn(norm_mlp, fc1_full) + vectors[4]
        below = 0.5 * (1.0 + lax.erf(preact * math.sqrt(0.5)))
        bell = jnp.exp(-0.5 * preact * preact) * (1.0 / math.sqrt(2.0 * math.pi))
        return (preact * below).astype(BF16), below + preact * bell

    rows_in = [boundary[0, k] for k in range(micro_count)]
    first_rows = bring(0, rows_in)
    qkv_half = split_qkv()
    (segment, position), (seg_keys, pos_keys) = find_places()
    other_vector = trade(own_vector)
    qkv_in0, position, other_vector, first_rows, fc1_weight, out_weight, fc2_weight = pin(
        repeat(qkv_half[0]), position, other_vector, first_rows, fc1_weight, out_weight, fc2_weight
    )
    qkv_dealt0 = exchange(qkv_in0)
    vectors = [cut_vector(vector) for vector in in_order(own_vector, other_vector)]
    fc1_half, push_half = split_fc1(), split_push()
    fc1_in0, push_in0 = repeat(fc1_half[0]), repeat(push_half[0])

    def pin_first(held):
        nonlocal qkv_dealt0, fc1_in0, push_in0
        qkv_dealt0, fc1_in0, push_in0, held = pin(qkv_dealt0, fc1_in0, push_in0, held)
        return held

    full0 = plan.spread(first_rows, [None, None, pin_first])

    fc1_dealt0 = exchange(fc1_in0)
    qkv0 = join_qkv(qkv_dealt0)
    norm_attn0, norm_mlp0 = norms(full0, vectors[0])
    fc1_dealt0, push_in0, norm_attn0, norm_mlp0, qkv0, rows_in = pin(
        fc1_dealt0, push_in0, norm_attn0, norm_mlp0, qkv0, rows_in
    )
    push_dealt0 = exchange(push_in0)
    allowed = (segment[:, None] == seg_keys[None, :]) & (pos_keys[None, :] <= position[:, None])
    cosine, sine_part = angles(position)
    queries0, keys0, values0 = project(norm_attn0, qkv0, vectors[0])
    grad1 = bring(1, rows_in)
    attended0, log_total0 = attend(queries0, keys0, values0)
    fc1_0 = join_fc1(fc1_dealt0)
    hidden0, slope0 = open_units(norm_mlp0, fc1_0, vectors[0])
    pushed0 = join_pushed(attended0, hidden0)
    grad_full1 = plan.spread(grad1)
    qkv_in1, fc1_in1, push_in1 = [repeat(half[1]) for half in (qkv_half, fc1_half, push_half)]
    pushed0, slope0, push_dealt0, grad_full1, qkv_in1, fc1_in1, push_in1 = pin(
        pushed0, slope0, push_dealt0, grad_full1, qkv_in1, fc1_in1, push_in1
    )
    qkv_dealt1 = exchange(qkv_in1)
    push0 = join_push(push_dealt0)
    middle_rows = add_branch(first_rows, plan.collect(push(pushed0, push0)), vectors[0])

    def pin_second(held):
        nonlocal qkv_dealt1, fc1_in1
        qkv_dealt1, fc1_in1, held = pin(qkv_dealt1, fc1_in1, held)
        return held

    full1 = plan.spread(middle_rows, [None, None, pin_second])

    fc1_dealt1 = exchange(fc1_in1)
    qkv1 = join_qkv(qkv_dealt1)
    norm_attn1, norm_mlp1 = norms(full1, vectors[1])
    queries1, keys1, values1 = project(norm_attn1, qkv1, vectors[1])
    fc1_dealt1, push_in1, queries1, keys1 = pin(fc1_dealt1, push_in1, queries1, keys1)
    push_dealt1 = exchange(push_in1)
    attended1, log_total1 = attend(queries1, keys1, values1)
    fc1_1 = join_fc1(fc1_dealt1)
    hidden1, slope1 = open_units(norm_mlp1, fc1_1, vectors[1])
    pushed1 = join_pushed(attended1, hidden1)
    push_back1 = push_blocks(pushed1, grad_full1)
    push_dealt1, push_back1, slope1 = pin(push_dealt1, push_back1, slope1)
    push_came1 = exchange(push_back1)
    push1 = join_push(push_dealt1)
    d_attended1, d_hidden1 = cut_pushed(dot_nt(grad_full1, push1))
    d_preact1 = (d_hidden1 * slope1).astype(BF16)
    fc1_back1 = fc1_blocks(norm_mlp1, d_preact1)
    last_parts = push(pushed1, push1)
    d_projected1 = attend_back(queries1, keys1, values1, log_total1, d_attended1)
    d_scaled1, norm_sums1 = norm_grads(d_projected1, d_preact1, qkv1, fc1_1, full1, vectors[1])
    push_came1, fc1_back1, d_scaled1 = pin(push_came1, fc1_back1, d_scaled1)
    fc1_came1 = exchange(fc1_back1)
    grad0 = input_grad(grad1, middle_rows, plan.collect(plan.cut(d_scaled1)))
    qkv_back1 = qkv_blocks(norm_attn1, d_projected1)

    def pin_third(held):
        nonlocal fc1_came1, qkv_back1
        fc1_came1, qkv_back1, held = pin(fc1_came1, qkv_back1, held)
        return held

    grad_full0 = plan.spread(grad0, [None, None, pin_third])
    qkv_came1 = exchange(qkv_back1)

    push_back0 = push_blocks(pushed0, grad_full0)
    push_back0, grad_full0, qkv_came1, last_parts, norm_sums1 = pin(
        push_back0, grad_full0, qkv_came1, last_parts, norm_sums1
    )
    push_came0 = exchange(push_back0)
    d_attended0, d_hidden0 = cut_pushed(dot_nt(grad_full0, push0))
    d_preact0 = (d_hidden0 * slope0).astype(BF16)
    fc1_back0 = fc1_blocks(norm_mlp0, d_preact0)
    d_projected0 = attend_back(queries0, keys0, values0, log_total0, d_attended0)
    push_came0, fc1_back0, d_projected0, last_parts = pin(
        push_came0, fc1_back0, d_projected0, last_parts
    )
    fc1_came0 = exchange(fc1_back0)
    qkv_back0 = qkv_blocks(norm_attn0, d_projected0)
    d_scaled0, norm_sums0 = norm_grads(d_projected0, d_preact0, qkv0, fc1_0, full0, vectors[0])
    fc1_came0, qkv_back0, d_scaled0 = pin(fc1_came0, qkv_back0, d_scaled0)
    qkv_came0 = exchange(qkv_back0)
    d_rows0 = plan.collect(plan.cut(d_scaled0))
    last_rows = add_branch(middle_rows, plan.collect(last_parts), vectors[1])
    qkv_came0, last_rows, d_rows0 = pin(qkv_came0, last_rows, d_rows0)
    d_input = input_grad(grad0, first_rows, d_rows0)
    total = sum_everywhere(
        jnp.stack(
            [
                vector_sums(norm_sums0, d_projected0, d_preact0, grad0),
                vector_sums(norm_sums1, d_projected1, d_preact1, grad1),
            ]
        )
    )
    result = jnp.where(section == 0, take_home(d_input, 0), take_home(last_rows, 1))

    def finish(came0, came1):
        mine, yours = in_order(gather_sum(came0), gather_sum(came1))
        return jnp.stack(in_order(mine, trade(yours.astype(BF16)).astype(F32)))

    push_all = finish(push_came0, push_came1)
    fc1_all = finish(fc1_came0, fc1_came1)
    qkv_all = finish(qkv_came0, qkv_came1)
    qkv_out = (
        qkv_all.reshape(2, heads_here, depth, 3, half_head)
        .transpose(2, 3, 1, 0, 4)
        .reshape(depth, 3, heads_here * HD)
    )
    fc1_out = fc1_all.transpose(2, 1, 0, 3).reshape(depth, heads_here * units)
    out_out = push_all[:, :, :half_head].transpose(1, 0, 2, 3).reshape(heads_here * HD, depth)
    fc2_out = push_all[:, :, half_head:].transpose(1, 0, 2, 3).reshape(heads_here * units, depth)
    total = jnp.where(section == 0, total[0], total[1])
    return (
        result[None],
        qkv_out[None],
        out_out[None],
        fc1_out[None],
        fc2_out[None],
        total[: 2 * width].reshape(1, 2, width),
        total[2 * width : 4 * width].reshape(1, 2, width),
        total[5 * width : 8 * width].reshape(1, 3, width),
        total[8 * width :][None],
        jnp.broadcast_to(total[4 * width : 5 * width], (1, 2, width)),
    )


def solution(mesh):
    return jax.shard_map(
        per_device,
        mesh=mesh,
        in_specs=(
            P("section", None, ("context", "tensor"), None),
            P(None, "context"),
            P(),
            P("section", "context", None, "tensor"),
            P("section", "tensor", "context"),
            P("section", "context", "tensor"),
            P("section", "tensor", "context"),
            P("section", None, None),
            P("section", None, None),
            P("section", None, None),
            P("section", None),
            P("section", None, None),
        ),
        out_specs=(
            P("section", None, ("context", "tensor"), None),
            P("section", "context", None, "tensor"),
            P("section", "tensor", "context"),
            P("section", "context", "tensor"),
            P("section", "tensor", "context"),
            P("section", None, None),
            P("section", None, None),
            P("section", None, None),
            P("section", None),
            P("section", None, None),
        ),
        check_vma=False,
    )
```

```python
import math

import jax
import jax.numpy as jnp
import numpy as np
from jax import lax
from jax.sharding import PartitionSpec as P

HD = 256
ROT = 64

EPSILON = 1e-05
ROTARY_BASE = 10000.0
MASKED = -1e30

BF16 = jnp.bfloat16
F32 = jnp.float32


def locate(placed, lengths):
    seq_ends = jnp.cumsum(lengths)
    seq_starts = seq_ends - lengths
    segment = jnp.sum((placed[:, None] >= seq_ends[None, :]).astype(jnp.int32), axis=1)
    chosen = segment[:, None] == jnp.arange(lengths.shape[0], dtype=jnp.int32)[None, :]
    seq_begin = jnp.sum(jnp.where(chosen, seq_starts[None, :], 0), axis=1)
    return (segment, placed - seq_begin)


def normalize_parts(values):
    row_mean = jnp.mean(values, axis=-1, keepdims=True)
    centered = values - row_mean
    inv_std = lax.rsqrt(jnp.mean(centered * centered, axis=-1, keepdims=True) + EPSILON)
    return (centered * inv_std, inv_std)


def angles(position):
    half_rot = ROT // 2
    frequency = ROTARY_BASE ** (-(jnp.arange(half_rot, dtype=F32) * 2.0) / ROT)
    phase_angle = position.astype(F32)[:, None] * frequency[None, :]
    return (jnp.cos(phase_angle), jnp.sin(phase_angle))


def rotate_pairs(values, cosine, sine_part):
    half_rot = ROT // 2
    leading = values[:, :half_rot]
    second = values[:, half_rot:ROT]
    return jnp.concatenate(
        [
            leading * cosine - second * sine_part,
            second * cosine + leading * sine_part,
            values[:, ROT:],
        ],
        axis=-1,
    )


def dot_tn(left_side, right_side):
    return lax.dot_general(
        left_side, right_side, (((0,), (0,)), ((), ())), preferred_element_type=F32
    )


def dot_nt(left_side, right_side):
    return lax.dot_general(
        left_side, right_side, (((1,), (1,)), ((), ())), preferred_element_type=F32
    )


def dot_nn(left_side, right_side):
    return jnp.dot(left_side, right_side, preferred_element_type=F32)


def pin(*values):
    return lax.optimization_barrier(values)


def flip(value, axis, mask):
    count = lax.axis_size(axis)
    return lax.ppermute(value, axis, [(place, place ^ mask) for place in range(count)])


def trade(value):
    return flip(value, "section", 1)


class Plan:
    def __init__(self, micro_count, heads_here, part_rows):
        self.contexts = lax.axis_size("context")
        self.tensors = lax.axis_size("tensor")
        self.heads = heads_here
        self.span = self.contexts // micro_count
        self.shares = self.span // heads_here
        self.part_rows = part_rows
        self.section = lax.axis_index("section")
        self.context = lax.axis_index("context")
        self.tensor = lax.axis_index("tensor")
        self.micro = self.context // self.span
        self.share = (self.context % self.span) // heads_here
        self.head = self.context % heads_here
        bits = [("context", 1 << b) for b in range(int(math.log2(heads_here)))]
        bits += [("tensor", 1 << b) for b in range(int(math.log2(self.tensors)))]
        ways = len(bits)
        cuts = [8 * ((part_rows // 8 * k + ways - 1) // ways) for k in range(ways + 1)]
        self.chunks = [(cuts[k], cuts[k + 1] - cuts[k]) for k in range(ways)]
        self.orders = [bits[k:] + bits[:k] for k in range(ways)]
        self.partners = 1 << ways
        head_flip, tensor_flip, row = [], [], []
        for (start, rows), order in zip(self.chunks, self.orders):
            for block in range(self.partners):
                masks = {"context": 0, "tensor": 0}
                for place, (axis, mask) in enumerate(order):
                    if block >> place & 1:
                        masks[axis] |= mask
                head_flip += [masks["context"]] * rows
                tensor_flip += [masks["tensor"]] * rows
                row += list(range(start, start + rows))
        self.head_flip = np.array(head_flip, np.int32)
        self.tensor_flip = np.array(tensor_flip, np.int32)
        self.row = np.array(row, np.int32)
        self.rows = len(row)

    def cut(self, full):
        return [
            full[start * self.partners : (start + rows) * self.partners]
            for start, rows in self.chunks
        ]

    def spread(self, *owns, pins=()):
        held = [own[start : start + rows] for own in owns for start, rows in self.chunks]
        orders = self.orders * len(owns)
        steps = len(self.chunks)
        for step in range(steps):
            came = [flip(v, *order[step]) for v, order in zip(held, orders)]
            came = list(pins[step](came) if step < len(pins) else pin(*came))
            if step < steps - 1:
                held = [jnp.concatenate([v, w], axis=0) for v, w in zip(held, came)]
                held = list(pin(*held))
        pairs = [v for pair in zip(held, came) for v in pair]
        each = len(pairs) // len(owns)
        return [jnp.concatenate(pairs[k : k + each], axis=0) for k in range(0, len(pairs), each)]

    def collect(self, *sets, pins=()):
        held = [part for parts in sets for part in parts]
        orders = self.orders * len(sets)
        steps = len(self.chunks)
        for count, step in enumerate(reversed(range(steps))):
            came = [flip(v[v.shape[0] // 2 :], *order[step]) for v, order in zip(held, orders)]
            came = list(pins[count](came) if count < len(pins) else pin(*came))
            held = [v[: v.shape[0] // 2].astype(F32) + w.astype(F32) for v, w in zip(held, came)]
            if step:
                held = list(pin(*[v.astype(BF16) for v in held]))
        return [jnp.concatenate(held[k : k + steps], axis=0) for k in range(0, len(held), steps)]

    def heads_of(self, full):
        return [
            full[start * self.partners : start * self.partners + 2 * rows]
            for start, rows in self.chunks
        ]

    def own_of(self, pairs):
        return jnp.concatenate([v[: v.shape[0] // 2] for v in pairs], axis=0)

    def sum_and_spread(self, parts, mix, sum_pins=(), spread_pins=()):
        steps = len(self.chunks)
        held = list(parts)
        for count, step in enumerate(range(steps - 1, 0, -1)):
            came = self.send_half(held, step)
            came = list(sum_pins[count](came) if count < len(sum_pins) else pin(*came))
            held = list(pin(*self.add_half(held, came)))
        came = self.send(held, 0)
        came = list(sum_pins[steps - 1](came) if len(sum_pins) >= steps else pin(*came))
        pairs = []
        for which, (v, w) in enumerate(zip(held, came)):
            half = v.shape[0] // 2
            swapped = jnp.concatenate([w[half:], w[:half]], axis=0)
            pairs.append(mix(which, v.astype(F32) + swapped.astype(F32)))
        pairs = list(pin(*pairs))
        held = pairs
        for count, step in enumerate(range(1, steps)):
            came = self.send(held, step)
            came = list(spread_pins[count](came) if count < len(spread_pins) else pin(*came))
            if step < steps - 1:
                held = list(pin(*self.join(held, came)))
        return self.own_of(pairs), self.whole(held, came)

    def pieces(self, own):
        return [own[start : start + rows] for start, rows in self.chunks]

    def send(self, held, step):
        return [flip(v, *order[step]) for v, order in zip(held, self.orders)]

    def join(self, held, came):
        return [jnp.concatenate([v, w], axis=0) for v, w in zip(held, came)]

    def whole(self, held, came):
        return jnp.concatenate([v for pair in zip(held, came) for v in pair], axis=0)

    def send_half(self, held, step):
        return [flip(v[v.shape[0] // 2 :], *order[step]) for v, order in zip(held, self.orders)]

    def add_half(self, held, came):
        return [
            (v[: v.shape[0] // 2].astype(F32) + w.astype(F32)).astype(BF16)
            for v, w in zip(held, came)
        ]

    def rows_of(self, places, section, share):
        context = section * self.span + share * self.heads + (self.head ^ self.head_flip)
        chosen = context[:, None] == jnp.arange(self.contexts, dtype=jnp.int32)[None, :]
        first = jnp.sum(jnp.where(chosen, places[None, :], 0), axis=1)
        within = (self.tensor ^ self.tensor_flip) * self.part_rows + self.row
        return first + within * self.contexts


def per_device(
    boundary,
    token_places,
    lengths,
    qkv_weight,
    out_weight,
    fc1_weight,
    fc2_weight,
    norm_gain,
    norm_bias,
    qkv_bias,
    fc1_bias,
    branch_bias,
):
    micro_count, part_rows, width = boundary.shape[1:]
    depth = qkv_weight.shape[1]
    heads_here = qkv_weight.shape[3] // HD
    units = fc1_weight.shape[2] // heads_here
    all_units = fc1_bias.shape[1]
    plan = Plan(micro_count, heads_here, part_rows)
    section, span, contexts = plan.section, plan.span, plan.contexts
    half_head, half_units = HD // 2, units // 2
    half_push = half_head + half_units
    copies = micro_count * plan.shares
    score_scale = 1.0 / math.sqrt(HD)
    head_index = plan.tensor * heads_here + plan.head

    def in_order(own, other):
        return (jnp.where(section == 0, own, other), jnp.where(section == 0, other, own))

    def flat(place_section, place_context):
        return place_section * contexts + place_context

    def bring(origin, held):
        came = []
        for micro in range(micro_count):
            pairs = [
                (flat(origin, side * span + k), flat(side, micro * span + k))
                for side in range(micro_count)
                for k in range(span)
            ]
            came.append(lax.ppermute(held[micro], ("section", "context"), pairs))
        return jnp.where(plan.micro == 0, came[0], came[1])

    def take_home(own, target):
        came = []
        for micro in range(micro_count):
            pairs = [
                (flat(side, micro * span + k), flat(target, side * span + k))
                for side in range(micro_count)
                for k in range(span)
            ]
            came.append(lax.ppermute(own, ("section", "context"), pairs))
        return jnp.stack(came)

    def half_of(halves):
        kept = lax.dynamic_index_in_dim(halves, section, 0, keepdims=False)
        return kept, trade(lax.dynamic_index_in_dim(halves, 1 - section, 0, keepdims=False))

    def exchange(blocks):
        return lax.all_to_all(blocks, "context", split_axis=0, concat_axis=0, tiled=True)

    def repeat(half, layer):
        blocks = in_order(*half)[layer]
        spread = jnp.broadcast_to(blocks[None], (copies,) + blocks.shape)
        return spread.reshape((contexts,) + blocks.shape[1:])

    def split_qkv():
        blocks = qkv_weight[0].reshape(depth, 3, heads_here, 2, half_head)
        return half_of(blocks.transpose(3, 2, 0, 1, 4).reshape(2, heads_here, depth, 3 * half_head))

    def split_fc1():
        blocks = fc1_weight[0].reshape(depth, heads_here, 2, half_units)
        return half_of(blocks.transpose(2, 1, 0, 3))

    def split_push():
        blocks = jnp.concatenate(
            [
                out_weight[0].reshape(heads_here, 2, half_head, depth),
                fc2_weight[0].reshape(heads_here, 2, half_units, depth),
            ],
            axis=2,
        )
        return half_of(blocks.transpose(1, 0, 2, 3))

    def join_qkv(dealt):
        own = dealt.reshape(width, 3, half_head)
        low, high = in_order(own, trade(own))
        return jnp.stack([low, high], axis=2).reshape(width, 3 * HD)

    def join_fc1(dealt):
        own = dealt.reshape(width, half_units)
        return jnp.concatenate([own, trade(own)], axis=1)

    def join_push(dealt):
        own = dealt.transpose(1, 0, 2).reshape(half_push, width)
        return jnp.concatenate([own, trade(own)], axis=0)

    def gather_places():
        first = lax.all_gather(token_places[:, 0], "context", axis=0)
        return lax.dynamic_index_in_dim(first, plan.micro, 1, keepdims=False)

    def find_places(places):
        own_lengths = lax.dynamic_index_in_dim(lengths, plan.micro, 0, keepdims=False)
        own_spot = locate(plan.rows_of(places, section, plan.share), own_lengths)
        key_spots = [
            locate(plan.rows_of(places, section ^ side, plan.share ^ share), own_lengths)
            for side in range(2)
            for share in range(plan.shares)
        ]
        return own_spot, [jnp.concatenate(part) for part in zip(*key_spots)]

    def share_keys(value):
        held = [value]
        for share in range(1, plan.shares):
            held.append(flip(value, "context", share * heads_here))
        pile = jnp.concatenate(held, axis=0)
        return jnp.concatenate([pile, trade(pile)], axis=0)

    def return_keys(value):
        half = value.shape[0] // 2
        pile = value[:half] + trade(value[half:].astype(BF16)).astype(F32)
        total = pile[: plan.rows]
        for share in range(1, plan.shares):
            piece = pile[share * plan.rows : (share + 1) * plan.rows].astype(BF16)
            total = total + flip(piece, "context", share * heads_here).astype(F32)
        return total

    own_vector = jnp.concatenate(
        [
            norm_gain[0].reshape(-1),
            norm_bias[0].reshape(-1),
            branch_bias[0, 0] + branch_bias[0, 1],
            lax.dynamic_slice(qkv_bias[0], (0, head_index * HD), (3, HD)).reshape(-1),
            lax.dynamic_slice_in_dim(fc1_bias[0], head_index * units, units),
        ]
    )

    def unit_order(values):
        first, second = in_order(values[..., :half_units], values[..., half_units:])
        return jnp.concatenate([first, second], axis=-1)

    def cut_vector(vector):
        gain = vector[: 2 * width].reshape(2, width)
        bias = vector[2 * width : 4 * width].reshape(2, width)
        out_shift = vector[4 * width : 5 * width]
        qkv_shift = vector[5 * width : 5 * width + 3 * HD]
        return gain, bias, out_shift, qkv_shift, unit_order(vector[5 * width + 3 * HD :])

    def scaled_rows(full_rows):
        return normalize_parts(full_rows.astype(F32))[0]

    def norms(full_rows, vectors):
        gain, bias = vectors[:2]
        scaled = scaled_rows(full_rows)
        return [(scaled * gain[k] + bias[k]).astype(BF16) for k in range(2)]

    def project(norm_attn, qkv_full, vectors):
        projected = dot_nn(norm_attn, qkv_full) + vectors[3]
        queries = rotate_pairs(projected[:, :HD], cosine, sine_part).astype(BF16)
        key_rows = rotate_pairs(projected[:, HD : 2 * HD], cosine, sine_part).astype(BF16)
        value_rows = projected[:, 2 * HD :].astype(BF16)
        key_value = share_keys(jnp.concatenate([key_rows, value_rows], axis=1))
        return queries, key_value[:, :HD], key_value[:, HD:]

    def attend(queries, keys, values):
        scores = dot_nt(queries, keys) * score_scale
        masked = jnp.where(allowed, scores, MASKED)
        top = jnp.max(masked, axis=1, keepdims=True)
        weight = jnp.where(allowed, jnp.exp(masked - top), 0.0)
        probs = weight / jnp.sum(weight, axis=1, keepdims=True)
        return dot_nn(probs.astype(BF16), values).astype(BF16), probs

    def score_grads(values, probs, d_attended):
        d_probs = dot_nt(d_attended, values)
        centre = jnp.sum(probs * d_probs, axis=1, keepdims=True)
        return (probs * (d_probs - centre)).astype(BF16)

    def attend_back(queries, keys, probs, d_scores, d_attended):
        d_queries = dot_nn(d_scores, keys) * score_scale
        d_keys = dot_tn(d_scores, queries) * score_scale
        d_values = dot_tn(probs.astype(BF16), d_attended)
        key_grads = return_keys(jnp.concatenate([d_keys, d_values], axis=1))
        return jnp.concatenate(
            [
                rotate_pairs(d_queries, cosine, -sine_part),
                rotate_pairs(key_grads[:, :HD], cosine, -sine_part),
                key_grads[:, HD:],
            ],
            axis=1,
        ).astype(BF16)

    def join_pushed(attended, hidden):
        first, second = in_order(attended[:, :half_head], attended[:, half_head:])
        return jnp.concatenate(
            [first, hidden[:, :half_units], second, hidden[:, half_units:]], axis=1
        )

    def cut_pushed(d_pushed):
        first, second = in_order(
            d_pushed[:, :half_head], d_pushed[:, half_push : half_push + half_head]
        )
        d_attended = jnp.concatenate([first, second], axis=1).astype(BF16)
        d_hidden = jnp.concatenate(
            [d_pushed[:, half_head:half_push], d_pushed[:, half_push + half_head :]], axis=1
        )
        return d_attended, d_hidden

    def push(pushed, push_full):
        return [dot_nn(rows, push_full).astype(BF16) for rows in plan.cut(pushed)]

    def add_branch(own_rows, summed, vectors):
        return (own_rows.astype(F32) + summed + vectors[2]).astype(BF16)

    def sum_cores(rows, own, other):
        came = trade(dot_tn(rows, other).astype(BF16))
        return (dot_tn(rows, own) + came.astype(F32)).astype(BF16)

    def push_blocks(pushed, grad_full):
        came = trade(dot_tn(pushed[:, half_push:], grad_full).astype(BF16))
        half = (dot_tn(pushed[:, :half_push], grad_full) + came.astype(F32)).astype(BF16)
        return half.reshape(half_push, contexts, depth).transpose(1, 0, 2)

    def fc1_blocks(norm_mlp, d_preact):
        half = sum_cores(norm_mlp, d_preact[:, :half_units], d_preact[:, half_units:])
        return half.reshape(contexts, depth, half_units)

    def qkv_blocks(norm_attn, d_projected):
        parts = d_projected.reshape(plan.rows, 3, 2, half_head)
        own, other = in_order(parts[:, :, 0], parts[:, :, 1])
        shape = (plan.rows, 3 * half_head)
        half = sum_cores(norm_attn, own.reshape(shape), other.reshape(shape))
        return half.reshape(contexts, depth, 3 * half_head)

    def gather_sum(came):
        return jnp.sum(came.reshape((copies, heads_here) + came.shape[1:]).astype(F32), axis=0)

    def norm_grads(d_projected, d_preact, qkv_full, fc1_full, full_rows, vectors, pin=None):
        d_norm_attn = dot_nt(d_projected, qkv_full)
        if pin is not None:
            d_norm_attn, d_preact = pin(d_norm_attn, d_preact)
        d_norm_mlp = dot_nt(d_preact, fc1_full)
        gain = vectors[0]
        d_scaled = (d_norm_attn * gain[0] + d_norm_mlp * gain[1]).astype(BF16)
        scaled = scaled_rows(full_rows)
        sums = [
            jnp.sum(d_norm_attn * scaled, axis=0),
            jnp.sum(d_norm_mlp * scaled, axis=0),
            jnp.sum(d_norm_attn, axis=0),
            jnp.sum(d_norm_mlp, axis=0),
        ]
        return d_scaled, sums

    def input_grad(grad_own, own_rows, d_scaled):
        own_scaled, own_inv = normalize_parts(own_rows.astype(F32))
        d_input = grad_own.astype(F32) + own_inv * (
            d_scaled
            - jnp.mean(d_scaled, axis=-1, keepdims=True)
            - own_scaled * jnp.mean(d_scaled * own_scaled, axis=-1, keepdims=True)
        )
        return d_input.astype(BF16)

    def vector_sums(norm_sums, d_projected, d_preact, grad_own):
        qkv_part = lax.dynamic_update_slice(
            jnp.zeros((3, width), F32),
            jnp.sum(d_projected, axis=0, dtype=F32).reshape(3, HD),
            (0, head_index * HD),
        )
        unit_part = lax.dynamic_update_slice_in_dim(
            jnp.zeros((all_units,), F32),
            unit_order(jnp.sum(d_preact, axis=0, dtype=F32)),
            head_index * units,
            0,
        )
        return jnp.concatenate(
            norm_sums
            + [jnp.sum(grad_own.astype(F32), axis=0), qkv_part.reshape(-1), unit_part]
        )

    def open_units(norm_mlp, fc1_full, vectors):
        preact = dot_nn(norm_mlp, fc1_full) + vectors[4]
        below = 0.5 * (1.0 + lax.erf(preact * math.sqrt(0.5)))
        bell = jnp.exp(-0.5 * preact * preact) * (1.0 / math.sqrt(2.0 * math.pi))
        return (preact * below).astype(BF16), below + preact * bell

    def finish(came0, came1):
        mine, yours = in_order(gather_sum(came0), gather_sum(came1))
        return jnp.stack(in_order(mine, trade(yours.astype(BF16)).astype(F32)))

    rows_in = [boundary[0, k] for k in range(micro_count)]
    first_rows = bring(0, rows_in)
    first_rows, qkv_weight, places, own_vector = pin(
        first_rows, qkv_weight, gather_places(), own_vector
    )
    qkv_half = split_qkv()

    def pin_gather(came):
        nonlocal qkv_half, fc1_weight, out_weight, fc2_weight, own_vector, rows_in
        qkv_half, fc1_weight, out_weight, fc2_weight, own_vector, rows_in, came = pin(
            qkv_half, fc1_weight, out_weight, fc2_weight, own_vector, rows_in, came
        )
        return came

    full0 = plan.spread(first_rows, pins=[pin_gather])[0]
    qkv_in0 = repeat(qkv_half, 0)
    other_vector = trade(own_vector)
    grad1 = bring(1, rows_in)
    full0, qkv_in0, grad1, other_vector = pin(full0, qkv_in0, grad1, other_vector)
    (segment, position), (seg_keys, pos_keys) = find_places(places)
    fc1_half = split_fc1()
    fc1_in0 = repeat(fc1_half, 0)
    held1 = plan.pieces(grad1)
    vectors = [cut_vector(vector) for vector in in_order(own_vector, other_vector)]

    qkv_dealt0 = exchange(qkv_in0)
    norm_attn0, norm_mlp0 = norms(full0, vectors[0])
    push_half = split_push()
    qkv_dealt0, fc1_in0, push_half, norm_attn0, norm_mlp0, came1 = pin(
        qkv_dealt0, fc1_in0, push_half, norm_attn0, norm_mlp0, plan.send(held1, 0)
    )
    held1 = plan.join(held1, came1)
    fc1_dealt0 = exchange(fc1_in0)
    allowed = (segment[:, None] == seg_keys[None, :]) & (pos_keys[None, :] <= position[:, None])
    cosine, sine_part = angles(position)
    qkv0 = join_qkv(qkv_dealt0)
    queries0, keys0, values0 = project(norm_attn0, qkv0, vectors[0])
    push_in0 = repeat(push_half, 0)
    fc1_dealt0, push_in0, queries0, keys0, came1 = pin(
        fc1_dealt0, push_in0, queries0, keys0, plan.send(held1, 1)
    )
    held1 = plan.join(held1, came1)
    push_dealt0 = exchange(push_in0)
    attended0, probs0 = attend(queries0, keys0, values0)
    fc1_0 = join_fc1(fc1_dealt0)
    hidden0, slope0 = open_units(norm_mlp0, fc1_0, vectors[0])
    pushed0 = join_pushed(attended0, hidden0)
    qkv_in1, fc1_in1, push_in1 = [repeat(half, 1) for half in (qkv_half, fc1_half, push_half)]
    pushed0, probs0, slope0, push_dealt0, qkv_in1, fc1_in1, push_in1, came1 = pin(
        pushed0, probs0, slope0, push_dealt0, qkv_in1, fc1_in1, push_in1, plan.send(held1, 2)
    )
    grad_full1 = plan.whole(held1, came1)
    qkv_dealt1 = exchange(qkv_in1)
    push0 = join_push(push_dealt0)
    parts0 = push(pushed0, push0)
    qkv_dealt1, parts0 = pin(qkv_dealt1, parts0)
    heads0 = plan.heads_of(full0)
    middle_rows, full1 = plan.sum_and_spread(
        parts0, lambda which, summed: add_branch(heads0[which], summed, vectors[0])
    )

    full1, qkv_dealt1, fc1_in1 = pin(full1, qkv_dealt1, fc1_in1)
    fc1_dealt1 = exchange(fc1_in1)
    qkv1 = join_qkv(qkv_dealt1)
    norm_attn1, norm_mlp1 = norms(full1, vectors[1])
    queries1, keys1, values1 = project(norm_attn1, qkv1, vectors[1])
    fc1_dealt1, push_in1, queries1, keys1 = pin(fc1_dealt1, push_in1, queries1, keys1)
    push_dealt1 = exchange(push_in1)
    attended1, probs1 = attend(queries1, keys1, values1)
    fc1_1 = join_fc1(fc1_dealt1)
    hidden1, slope1 = open_units(norm_mlp1, fc1_1, vectors[1])
    pushed1 = join_pushed(attended1, hidden1)
    push_back1 = push_blocks(pushed1, grad_full1)
    push_dealt1, push_back1, slope1, probs1 = pin(push_dealt1, push_back1, slope1, probs1)
    push_came1 = exchange(push_back1)
    push1 = join_push(push_dealt1)
    d_attended1, d_hidden1 = cut_pushed(dot_nt(grad_full1, push1))
    d_preact1 = (d_hidden1 * slope1).astype(BF16)
    fc1_back1 = fc1_blocks(norm_mlp1, d_preact1)
    d_scores1 = score_grads(values1, probs1, d_attended1)
    d_projected1 = attend_back(queries1, keys1, probs1, d_scores1, d_attended1)
    push_came1, fc1_back1, d_projected1 = pin(push_came1, fc1_back1, d_projected1)
    fc1_came1 = exchange(fc1_back1)
    d_scaled1, norm_sums1 = norm_grads(d_projected1, d_preact1, qkv1, fc1_1, full1, vectors[1])
    parts1 = plan.cut(d_scaled1)

    def pin_third(held):
        nonlocal fc1_came1
        fc1_came1, held = pin(fc1_came1, held)
        return held

    qkv_back1 = qkv_blocks(norm_attn1, d_projected1)
    last_parts = []

    def pin_push(came):
        nonlocal pushed1
        which = len(last_parts)
        part = dot_nn(plan.cut(pushed1)[which], push1).astype(BF16)
        part, pushed1, came = pin(part, pushed1, came)
        last_parts.append(part)
        return came

    grad_heads1, heads1 = plan.heads_of(grad_full1), plan.heads_of(full1)
    grad0, grad_full0 = plan.sum_and_spread(
        parts1,
        lambda which, summed: input_grad(grad_heads1[which], heads1[which], summed),
        [pin_third, pin_push, pin_push],
        [pin_push],
    )
    total1 = vector_sums(norm_sums1, d_projected1, d_preact1, grad1)

    grad_full0, qkv_back1, total1 = pin(grad_full0, qkv_back1, total1)
    total1 = lax.psum(total1, ("section", "context", "tensor"))
    qkv_came1 = exchange(qkv_back1)
    push_back0 = push_blocks(pushed0, grad_full0)
    push_back0, grad_full0, qkv_came1 = pin(push_back0, grad_full0, qkv_came1)
    push_came0 = exchange(push_back0)
    d_attended0, d_hidden0 = cut_pushed(dot_nt(grad_full0, push0))
    d_preact0 = (d_hidden0 * slope0).astype(BF16)
    fc1_back0 = fc1_blocks(norm_mlp0, d_preact0)
    d_scores0 = score_grads(values0, probs0, d_attended0)
    push_came0, fc1_back0, d_scores0, came = pin(
        push_came0, fc1_back0, d_scores0, plan.send_half(last_parts, 2)
    )
    last_parts = plan.add_half(last_parts, came)
    fc1_came0 = exchange(fc1_back0)
    d_projected0 = attend_back(queries0, keys0, probs0, d_scores0, d_attended0)
    qkv_back0 = qkv_blocks(norm_attn0, d_projected0)
    d_scaled0, norm_sums0 = norm_grads(d_projected0, d_preact0, qkv0, fc1_0, full0, vectors[0])
    fc1_came0, qkv_back0, d_scaled0, norm_sums0, push_came0, push_came1, came = pin(
        fc1_came0,
        qkv_back0,
        d_scaled0,
        norm_sums0,
        push_came0,
        push_came1,
        plan.send_half(last_parts, 1),
    )
    last_parts = plan.add_half(last_parts, came)
    qkv_came0 = exchange(qkv_back0)
    push_all = finish(push_came0, push_came1)
    fc1_all = finish(fc1_came0, fc1_came1)
    fc1_out = fc1_all.transpose(2, 1, 0, 3).reshape(depth, heads_here * units)
    out_out = push_all[:, :, :half_head].transpose(1, 0, 2, 3).reshape(heads_here * HD, depth)
    fc2_out = push_all[:, :, half_head:].transpose(1, 0, 2, 3).reshape(heads_here * units, depth)
    total = vector_sums(norm_sums0, d_projected0, d_preact0, grad0)
    sums = [
        (axis, 1 << b)
        for axis in ("section", "tensor", "context")
        for b in range(int(math.log2(lax.axis_size(axis))))
    ]
    qkv_came0, fc1_out, out_out, fc2_out, total1, other, parts0 = pin(
        qkv_came0,
        fc1_out,
        out_out,
        fc2_out,
        total1,
        flip(total, *sums.pop(0)),
        plan.cut(d_scaled0),
    )
    total = total + other
    qkv_sums = in_order(gather_sum(qkv_came0), gather_sum(qkv_came1))
    qkv_other = last_home = None

    def pin_sum(came):
        nonlocal total, qkv_other, last_home
        other = flip(total, *sums.pop(0))
        if last_home is None:
            last_came, other, came = pin(plan.send_half(last_parts, 0), other, came)
            last_sum = [
                v[: v.shape[0] // 2].astype(F32) + w.astype(F32)
                for v, w in zip(last_parts, last_came)
            ]
            last_rows = add_branch(middle_rows, jnp.concatenate(last_sum, axis=0), vectors[1])
            last_home = take_home(last_rows, 1)
        elif qkv_other is None:
            qkv_other, last_home, other, came = pin(
                trade(qkv_sums[1].astype(BF16)), last_home, other, came
            )
        else:
            other, came = pin(other, came)
        total = total + other
        return came

    d_rows0 = plan.collect(parts0, pins=[pin_sum] * len(plan.chunks))[0]
    d_input = input_grad(grad0, first_rows, d_rows0)
    first_home, other = pin(take_home(d_input, 0), flip(total, *sums.pop(0)))
    total = total + other
    for spot in sums:
        total = total + flip(total, *spot)
    qkv_out = (
        jnp.stack(in_order(qkv_sums[0], qkv_other.astype(F32)))
        .reshape(2, heads_here, depth, 3, half_head)
        .transpose(2, 3, 1, 0, 4)
        .reshape(depth, 3, heads_here * HD)
    )
    first_home, total, last_home = pin(first_home, total, last_home)
    result = jnp.where(section == 0, first_home, last_home)
    total = jnp.where(section == 0, total, total1)
    return (
        result[None],
        qkv_out[None],
        out_out[None],
        fc1_out[None],
        fc2_out[None],
        total[: 2 * width].reshape(1, 2, width),
        total[2 * width : 4 * width].reshape(1, 2, width),
        total[5 * width : 8 * width].reshape(1, 3, width),
        total[8 * width :][None],
        jnp.broadcast_to(total[4 * width : 5 * width], (1, 2, width)),
    )


def solution(mesh):
    return jax.shard_map(
        per_device,
        mesh=mesh,
        in_specs=(
            P("section", None, ("context", "tensor"), None),
            P(None, "context"),
            P(),
            P("section", "context", None, "tensor"),
            P("section", "tensor", "context"),
            P("section", "context", "tensor"),
            P("section", "tensor", "context"),
            P("section", None, None),
            P("section", None, None),
            P("section", None, None),
            P("section", None),
            P("section", None, None),
        ),
        out_specs=(
            P("section", None, ("context", "tensor"), None),
            P("section", "context", None, "tensor"),
            P("section", "tensor", "context"),
            P("section", "context", "tensor"),
            P("section", "tensor", "context"),
            P("section", None, None),
            P("section", None, None),
            P("section", None, None),
            P("section", None),
            P("section", None, None),
        ),
        check_vma=False,
    )
```

```python
import math

import jax
import jax.numpy as jnp
import numpy as np
from jax import lax
from jax.sharding import PartitionSpec as P

HD = 256
ROT = 64

EPSILON = 1e-05
ROTARY_BASE = 10000.0
MASKED = -1e30

BF16 = jnp.bfloat16
F32 = jnp.float32


def locate(placed, lengths):
    seq_ends = jnp.cumsum(lengths)
    seq_starts = seq_ends - lengths
    segment = jnp.sum((placed[:, None] >= seq_ends[None, :]).astype(jnp.int32), axis=1)
    chosen = segment[:, None] == jnp.arange(lengths.shape[0], dtype=jnp.int32)[None, :]
    seq_begin = jnp.sum(jnp.where(chosen, seq_starts[None, :], 0), axis=1)
    return (segment, placed - seq_begin)


def normalize_parts(values):
    row_mean = jnp.mean(values, axis=-1, keepdims=True)
    centered = values - row_mean
    inv_std = lax.rsqrt(jnp.mean(centered * centered, axis=-1, keepdims=True) + EPSILON)
    return (centered * inv_std, inv_std)


def angles(position):
    half_rot = ROT // 2
    frequency = ROTARY_BASE ** (-(jnp.arange(half_rot, dtype=F32) * 2.0) / ROT)
    phase_angle = position.astype(F32)[:, None] * frequency[None, :]
    return (jnp.cos(phase_angle), jnp.sin(phase_angle))


def rotate_pairs(values, cosine, sine_part):
    half_rot = ROT // 2
    leading = values[:, :half_rot]
    second = values[:, half_rot:ROT]
    return jnp.concatenate(
        [
            leading * cosine - second * sine_part,
            second * cosine + leading * sine_part,
            values[:, ROT:],
        ],
        axis=-1,
    )


def dot_tn(left_side, right_side):
    return lax.dot_general(
        left_side, right_side, (((0,), (0,)), ((), ())), preferred_element_type=F32
    )


def dot_nt(left_side, right_side):
    return lax.dot_general(
        left_side, right_side, (((1,), (1,)), ((), ())), preferred_element_type=F32
    )


def dot_nn(left_side, right_side):
    return jnp.dot(left_side, right_side, preferred_element_type=F32)


def pin(*values):
    return lax.optimization_barrier(values)


def flip(value, axis, mask):
    count = lax.axis_size(axis)
    return lax.ppermute(value, axis, [(place, place ^ mask) for place in range(count)])


def trade(value):
    return flip(value, "section", 1)


class Plan:
    def __init__(self, micro_count, heads_here, part_rows):
        self.contexts = lax.axis_size("context")
        self.tensors = lax.axis_size("tensor")
        self.heads = heads_here
        self.span = self.contexts // micro_count
        self.shares = self.span // heads_here
        self.part_rows = part_rows
        self.section = lax.axis_index("section")
        self.context = lax.axis_index("context")
        self.tensor = lax.axis_index("tensor")
        self.micro = self.context // self.span
        self.share = (self.context % self.span) // heads_here
        self.head = self.context % heads_here
        bits = [("context", 1 << b) for b in range(int(math.log2(heads_here)))]
        bits += [("tensor", 1 << b) for b in range(int(math.log2(self.tensors)))]
        ways = len(bits)
        cuts = [8 * ((part_rows // 8 * k + ways - 1) // ways) for k in range(ways + 1)]
        self.chunks = [(cuts[k], cuts[k + 1] - cuts[k]) for k in range(ways)]
        self.orders = [bits[k:] + bits[:k] for k in range(ways)]
        self.partners = 1 << ways
        head_flip, tensor_flip, row = [], [], []
        for (start, rows), order in zip(self.chunks, self.orders):
            for block in range(self.partners):
                masks = {"context": 0, "tensor": 0}
                for place, (axis, mask) in enumerate(order):
                    if block >> place & 1:
                        masks[axis] |= mask
                head_flip += [masks["context"]] * rows
                tensor_flip += [masks["tensor"]] * rows
                row += list(range(start, start + rows))
        self.head_flip = np.array(head_flip, np.int32)
        self.tensor_flip = np.array(tensor_flip, np.int32)
        self.row = np.array(row, np.int32)
        self.rows = len(row)

    def cut(self, full):
        return [
            full[start * self.partners : (start + rows) * self.partners]
            for start, rows in self.chunks
        ]

    def spread(self, *owns, pins=()):
        held = [own[start : start + rows] for own in owns for start, rows in self.chunks]
        orders = self.orders * len(owns)
        steps = len(self.chunks)
        for step in range(steps):
            came = [flip(v, *order[step]) for v, order in zip(held, orders)]
            came = list(pins[step](came) if step < len(pins) else pin(*came))
            if step < steps - 1:
                held = [jnp.concatenate([v, w], axis=0) for v, w in zip(held, came)]
                held = list(pin(*held))
        pairs = [v for pair in zip(held, came) for v in pair]
        each = len(pairs) // len(owns)
        return [jnp.concatenate(pairs[k : k + each], axis=0) for k in range(0, len(pairs), each)]

    def collect(self, *sets, pins=()):
        held = [part for parts in sets for part in parts]
        orders = self.orders * len(sets)
        steps = len(self.chunks)
        for count, step in enumerate(reversed(range(steps))):
            came = [flip(v[v.shape[0] // 2 :], *order[step]) for v, order in zip(held, orders)]
            came = list(pins[count](came) if count < len(pins) else pin(*came))
            held = [v[: v.shape[0] // 2].astype(F32) + w.astype(F32) for v, w in zip(held, came)]
            if step:
                held = list(pin(*[v.astype(BF16) for v in held]))
        return [jnp.concatenate(held[k : k + steps], axis=0) for k in range(0, len(held), steps)]

    def heads_of(self, full):
        return [
            full[start * self.partners : start * self.partners + 2 * rows]
            for start, rows in self.chunks
        ]

    def own_of(self, pairs):
        return jnp.concatenate([v[: v.shape[0] // 2] for v in pairs], axis=0)

    def sum_and_spread(self, parts, mix, sum_pins=(), spread_pins=()):
        steps = len(self.chunks)
        held = list(parts)
        for count, step in enumerate(range(steps - 1, 0, -1)):
            came = self.send_half(held, step)
            came = list(sum_pins[count](came) if count < len(sum_pins) else pin(*came))
            held = list(pin(*self.add_half(held, came)))
        came = self.send(held, 0)
        came = list(sum_pins[steps - 1](came) if len(sum_pins) >= steps else pin(*came))
        pairs = []
        for which, (v, w) in enumerate(zip(held, came)):
            half = v.shape[0] // 2
            swapped = jnp.concatenate([w[half:], w[:half]], axis=0)
            pairs.append(mix(which, v.astype(F32) + swapped.astype(F32)))
        pairs = list(pin(*pairs))
        held = pairs
        for count, step in enumerate(range(1, steps)):
            came = self.send(held, step)
            came = list(spread_pins[count](came) if count < len(spread_pins) else pin(*came))
            if step < steps - 1:
                held = list(pin(*self.join(held, came)))
        return self.own_of(pairs), self.whole(held, came)

    def pieces(self, own):
        return [own[start : start + rows] for start, rows in self.chunks]

    def send(self, held, step):
        return [flip(v, *order[step]) for v, order in zip(held, self.orders)]

    def join(self, held, came):
        return [jnp.concatenate([v, w], axis=0) for v, w in zip(held, came)]

    def whole(self, held, came):
        return jnp.concatenate([v for pair in zip(held, came) for v in pair], axis=0)

    def send_half(self, held, step):
        return [flip(v[v.shape[0] // 2 :], *order[step]) for v, order in zip(held, self.orders)]

    def add_half(self, held, came):
        return [
            (v[: v.shape[0] // 2].astype(F32) + w.astype(F32)).astype(BF16)
            for v, w in zip(held, came)
        ]

    def rows_of(self, places, section, share):
        context = section * self.span + share * self.heads + (self.head ^ self.head_flip)
        chosen = context[:, None] == jnp.arange(self.contexts, dtype=jnp.int32)[None, :]
        first = jnp.sum(jnp.where(chosen, places[None, :], 0), axis=1)
        within = (self.tensor ^ self.tensor_flip) * self.part_rows + self.row
        return first + within * self.contexts


def per_device(
    boundary,
    token_places,
    lengths,
    qkv_weight,
    out_weight,
    fc1_weight,
    fc2_weight,
    norm_gain,
    norm_bias,
    qkv_bias,
    fc1_bias,
    branch_bias,
):
    micro_count, part_rows, width = boundary.shape[1:]
    depth = qkv_weight.shape[1]
    heads_here = qkv_weight.shape[3] // HD
    units = fc1_weight.shape[2] // heads_here
    all_units = fc1_bias.shape[1]
    plan = Plan(micro_count, heads_here, part_rows)
    section, span, contexts = plan.section, plan.span, plan.contexts
    half_head, half_units = HD // 2, units // 2
    half_push = half_head + half_units
    copies = micro_count * plan.shares
    score_scale = 1.0 / math.sqrt(HD)
    head_index = plan.tensor * heads_here + plan.head

    def in_order(own, other):
        return (jnp.where(section == 0, own, other), jnp.where(section == 0, other, own))

    def flat(place_section, place_context):
        return place_section * contexts + place_context

    def bring(origin, held):
        came = []
        for micro in range(micro_count):
            pairs = [
                (flat(origin, side * span + k), flat(side, micro * span + k))
                for side in range(micro_count)
                for k in range(span)
            ]
            came.append(lax.ppermute(held[micro], ("section", "context"), pairs))
        return jnp.where(plan.micro == 0, came[0], came[1])

    def take_home(own, target):
        came = []
        for micro in range(micro_count):
            pairs = [
                (flat(side, micro * span + k), flat(target, side * span + k))
                for side in range(micro_count)
                for k in range(span)
            ]
            came.append(lax.ppermute(own, ("section", "context"), pairs))
        return jnp.stack(came)

    def half_of(halves):
        kept = lax.dynamic_index_in_dim(halves, section, 0, keepdims=False)
        return kept, trade(lax.dynamic_index_in_dim(halves, 1 - section, 0, keepdims=False))

    def exchange(blocks):
        return lax.all_to_all(blocks, "context", split_axis=0, concat_axis=0, tiled=True)

    def repeat(half, layer):
        blocks = in_order(*half)[layer]
        spread = jnp.broadcast_to(blocks[None], (copies,) + blocks.shape)
        return spread.reshape((contexts,) + blocks.shape[1:])

    def split_qkv():
        blocks = qkv_weight[0].reshape(depth, 3, heads_here, 2, half_head)
        return half_of(blocks.transpose(3, 2, 0, 1, 4).reshape(2, heads_here, depth, 3 * half_head))

    def split_fc1():
        blocks = fc1_weight[0].reshape(depth, heads_here, 2, half_units)
        return half_of(blocks.transpose(2, 1, 0, 3))

    def split_push():
        blocks = jnp.concatenate(
            [
                out_weight[0].reshape(heads_here, 2, half_head, depth),
                fc2_weight[0].reshape(heads_here, 2, half_units, depth),
            ],
            axis=2,
        )
        return half_of(blocks.transpose(1, 0, 2, 3))

    def join_qkv(dealt):
        own = dealt.reshape(width, 3, half_head)
        low, high = in_order(own, trade(own))
        return jnp.stack([low, high], axis=2).reshape(width, 3 * HD)

    def join_fc1(dealt):
        own = dealt.reshape(width, half_units)
        return jnp.concatenate([own, trade(own)], axis=1)

    def join_push(dealt):
        own = dealt.transpose(1, 0, 2).reshape(half_push, width)
        return jnp.concatenate([own, trade(own)], axis=0)

    def gather_places():
        first = lax.all_gather(token_places[:, 0], "context", axis=0)
        return lax.dynamic_index_in_dim(first, plan.micro, 1, keepdims=False)

    def find_places(places):
        own_lengths = lax.dynamic_index_in_dim(lengths, plan.micro, 0, keepdims=False)
        own_spot = locate(plan.rows_of(places, section, plan.share), own_lengths)
        key_spots = [
            locate(plan.rows_of(places, section ^ side, plan.share ^ share), own_lengths)
            for side in range(2)
            for share in range(plan.shares)
        ]
        return own_spot, [jnp.concatenate(part) for part in zip(*key_spots)]

    def share_keys(value):
        held = [value]
        for share in range(1, plan.shares):
            held.append(flip(value, "context", share * heads_here))
        pile = jnp.concatenate(held, axis=0)
        return jnp.concatenate([pile, trade(pile)], axis=0)

    def return_keys(value):
        half = value.shape[0] // 2
        pile = value[:half] + trade(value[half:].astype(BF16)).astype(F32)
        total = pile[: plan.rows]
        for share in range(1, plan.shares):
            piece = pile[share * plan.rows : (share + 1) * plan.rows].astype(BF16)
            total = total + flip(piece, "context", share * heads_here).astype(F32)
        return total

    own_vector = jnp.concatenate(
        [
            norm_gain[0].reshape(-1),
            norm_bias[0].reshape(-1),
            branch_bias[0, 0] + branch_bias[0, 1],
            lax.dynamic_slice(qkv_bias[0], (0, head_index * HD), (3, HD)).reshape(-1),
            lax.dynamic_slice_in_dim(fc1_bias[0], head_index * units, units),
        ]
    )

    def unit_order(values):
        first, second = in_order(values[..., :half_units], values[..., half_units:])
        return jnp.concatenate([first, second], axis=-1)

    def cut_vector(vector):
        gain = vector[: 2 * width].reshape(2, width)
        bias = vector[2 * width : 4 * width].reshape(2, width)
        out_shift = vector[4 * width : 5 * width]
        qkv_shift = vector[5 * width : 5 * width + 3 * HD]
        return gain, bias, out_shift, qkv_shift, unit_order(vector[5 * width + 3 * HD :])

    def scaled_rows(full_rows):
        return normalize_parts(full_rows.astype(F32))[0]

    def norms(full_rows, vectors):
        gain, bias = vectors[:2]
        scaled = scaled_rows(full_rows)
        return [(scaled * gain[k] + bias[k]).astype(BF16) for k in range(2)]

    def project(norm_attn, qkv_full, vectors):
        projected = dot_nn(norm_attn, qkv_full) + vectors[3]
        queries = rotate_pairs(projected[:, :HD], cosine, sine_part).astype(BF16)
        key_rows = rotate_pairs(projected[:, HD : 2 * HD], cosine, sine_part).astype(BF16)
        value_rows = projected[:, 2 * HD :].astype(BF16)
        key_value = share_keys(jnp.concatenate([key_rows, value_rows], axis=1))
        return queries, key_value[:, :HD], key_value[:, HD:]

    def attend(queries, keys, values):
        scores = dot_nt(queries, keys) * score_scale
        masked = jnp.where(allowed, scores, MASKED)
        top = jnp.max(masked, axis=1, keepdims=True)
        weight = jnp.where(allowed, jnp.exp(masked - top), 0.0)
        probs = weight / jnp.sum(weight, axis=1, keepdims=True)
        return dot_nn(probs.astype(BF16), values).astype(BF16), probs

    def score_grads(values, probs, d_attended):
        d_probs = dot_nt(d_attended, values)
        centre = jnp.sum(probs * d_probs, axis=1, keepdims=True)
        return (probs * (d_probs - centre)).astype(BF16)

    def attend_back(queries, keys, probs, d_scores, d_attended):
        d_queries = dot_nn(d_scores, keys) * score_scale
        d_keys = dot_tn(d_scores, queries) * score_scale
        d_values = dot_tn(probs.astype(BF16), d_attended)
        key_grads = return_keys(jnp.concatenate([d_keys, d_values], axis=1))
        return jnp.concatenate(
            [
                rotate_pairs(d_queries, cosine, -sine_part),
                rotate_pairs(key_grads[:, :HD], cosine, -sine_part),
                key_grads[:, HD:],
            ],
            axis=1,
        ).astype(BF16)

    def join_pushed(attended, hidden):
        first, second = in_order(attended[:, :half_head], attended[:, half_head:])
        return jnp.concatenate(
            [first, hidden[:, :half_units], second, hidden[:, half_units:]], axis=1
        )

    def cut_pushed(d_pushed):
        first, second = in_order(
            d_pushed[:, :half_head], d_pushed[:, half_push : half_push + half_head]
        )
        d_attended = jnp.concatenate([first, second], axis=1).astype(BF16)
        d_hidden = jnp.concatenate(
            [d_pushed[:, half_head:half_push], d_pushed[:, half_push + half_head :]], axis=1
        )
        return d_attended, d_hidden

    def push(pushed, push_full):
        return [dot_nn(rows, push_full).astype(BF16) for rows in plan.cut(pushed)]

    def add_branch(own_rows, summed, vectors):
        return (own_rows.astype(F32) + summed + vectors[2]).astype(BF16)

    def sum_cores(rows, own, other):
        came = trade(dot_tn(rows, other).astype(BF16))
        return (dot_tn(rows, own) + came.astype(F32)).astype(BF16)

    def push_blocks(pushed, grad_full):
        came = trade(dot_tn(pushed[:, half_push:], grad_full).astype(BF16))
        half = (dot_tn(pushed[:, :half_push], grad_full) + came.astype(F32)).astype(BF16)
        return half.reshape(half_push, contexts, depth).transpose(1, 0, 2)

    def fc1_blocks(norm_mlp, d_preact):
        half = sum_cores(norm_mlp, d_preact[:, :half_units], d_preact[:, half_units:])
        return half.reshape(contexts, depth, half_units)

    def qkv_blocks(norm_attn, d_projected):
        parts = d_projected.reshape(plan.rows, 3, 2, half_head)
        own, other = in_order(parts[:, :, 0], parts[:, :, 1])
        shape = (plan.rows, 3 * half_head)
        half = sum_cores(norm_attn, own.reshape(shape), other.reshape(shape))
        return half.reshape(contexts, depth, 3 * half_head)

    def gather_sum(came):
        return jnp.sum(came.reshape((copies, heads_here) + came.shape[1:]).astype(F32), axis=0)

    def norm_grads(d_projected, d_preact, qkv_full, fc1_full, full_rows, vectors, pin=None):
        d_norm_attn = dot_nt(d_projected, qkv_full)
        if pin is not None:
            d_norm_attn, d_preact = pin(d_norm_attn, d_preact)
        d_norm_mlp = dot_nt(d_preact, fc1_full)
        gain = vectors[0]
        d_scaled = (d_norm_attn * gain[0] + d_norm_mlp * gain[1]).astype(BF16)
        scaled = scaled_rows(full_rows)
        sums = [
            jnp.sum(d_norm_attn * scaled, axis=0),
            jnp.sum(d_norm_mlp * scaled, axis=0),
            jnp.sum(d_norm_attn, axis=0),
            jnp.sum(d_norm_mlp, axis=0),
        ]
        return d_scaled, sums

    def input_grad(grad_own, own_rows, d_scaled):
        own_scaled, own_inv = normalize_parts(own_rows.astype(F32))
        d_input = grad_own.astype(F32) + own_inv * (
            d_scaled
            - jnp.mean(d_scaled, axis=-1, keepdims=True)
            - own_scaled * jnp.mean(d_scaled * own_scaled, axis=-1, keepdims=True)
        )
        return d_input.astype(BF16)

    def vector_sums(norm_sums, d_projected, d_preact, grad_own):
        qkv_part = lax.dynamic_update_slice(
            jnp.zeros((3, width), F32),
            jnp.sum(d_projected, axis=0, dtype=F32).reshape(3, HD),
            (0, head_index * HD),
        )
        unit_part = lax.dynamic_update_slice_in_dim(
            jnp.zeros((all_units,), F32),
            unit_order(jnp.sum(d_preact, axis=0, dtype=F32)),
            head_index * units,
            0,
        )
        return jnp.concatenate(
            norm_sums
            + [jnp.sum(grad_own.astype(F32), axis=0), qkv_part.reshape(-1), unit_part]
        )

    def open_units(norm_mlp, fc1_full, vectors):
        preact = dot_nn(norm_mlp, fc1_full) + vectors[4]
        below = 0.5 * (1.0 + lax.erf(preact * math.sqrt(0.5)))
        bell = jnp.exp(-0.5 * preact * preact) * (1.0 / math.sqrt(2.0 * math.pi))
        return (preact * below).astype(BF16), below + preact * bell

    def finish(came0, came1):
        mine, yours = in_order(gather_sum(came0), gather_sum(came1))
        return jnp.stack(in_order(mine, trade(yours.astype(BF16)).astype(F32)))

    rows_in = [boundary[0, k] for k in range(micro_count)]
    first_rows = bring(0, rows_in)
    first_rows, qkv_weight, places, own_vector = pin(
        first_rows, qkv_weight, gather_places(), own_vector
    )
    qkv_half = split_qkv()

    def pin_gather(came):
        nonlocal qkv_half, own_vector, rows_in
        qkv_half, own_vector, rows_in, came = pin(qkv_half, own_vector, rows_in, came)
        return came

    full0 = plan.spread(first_rows, pins=[pin_gather])[0]
    qkv_in0 = repeat(qkv_half, 0)
    other_vector = trade(own_vector)
    grad1 = bring(1, rows_in)
    full0, qkv_in0, grad1, other_vector, fc1_weight, out_weight, fc2_weight = pin(
        full0, qkv_in0, grad1, other_vector, fc1_weight, out_weight, fc2_weight
    )
    (segment, position), (seg_keys, pos_keys) = find_places(places)
    fc1_half = split_fc1()
    fc1_in0 = repeat(fc1_half, 0)
    held1 = plan.pieces(grad1)
    vectors = [cut_vector(vector) for vector in in_order(own_vector, other_vector)]

    qkv_dealt0 = exchange(qkv_in0)
    norm_attn0, norm_mlp0 = norms(full0, vectors[0])
    push_half = split_push()
    qkv_dealt0, fc1_in0, push_half, norm_attn0, norm_mlp0, came1 = pin(
        qkv_dealt0, fc1_in0, push_half, norm_attn0, norm_mlp0, plan.send(held1, 0)
    )
    held1 = plan.join(held1, came1)
    fc1_dealt0 = exchange(fc1_in0)
    allowed = (segment[:, None] == seg_keys[None, :]) & (pos_keys[None, :] <= position[:, None])
    cosine, sine_part = angles(position)
    qkv0 = join_qkv(qkv_dealt0)
    queries0, keys0, values0 = project(norm_attn0, qkv0, vectors[0])
    push_in0 = repeat(push_half, 0)
    fc1_dealt0, push_in0, queries0, keys0, came1 = pin(
        fc1_dealt0, push_in0, queries0, keys0, plan.send(held1, 1)
    )
    held1 = plan.join(held1, came1)
    push_dealt0 = exchange(push_in0)
    attended0, probs0 = attend(queries0, keys0, values0)
    fc1_0 = join_fc1(fc1_dealt0)
    hidden0, slope0 = open_units(norm_mlp0, fc1_0, vectors[0])
    pushed0 = join_pushed(attended0, hidden0)
    qkv_in1, fc1_in1, push_in1 = [repeat(half, 1) for half in (qkv_half, fc1_half, push_half)]
    pushed0, probs0, slope0, push_dealt0, qkv_in1, fc1_in1, push_in1, came1 = pin(
        pushed0, probs0, slope0, push_dealt0, qkv_in1, fc1_in1, push_in1, plan.send(held1, 2)
    )
    grad_full1 = plan.whole(held1, came1)
    qkv_dealt1 = exchange(qkv_in1)
    push0 = join_push(push_dealt0)
    parts0 = push(pushed0, push0)

    def pin_deal(came):
        nonlocal qkv_dealt1
        qkv_dealt1, came = pin(qkv_dealt1, came)
        return came

    heads0 = plan.heads_of(full0)
    middle_rows, full1 = plan.sum_and_spread(
        parts0, lambda which, summed: add_branch(heads0[which], summed, vectors[0]), [pin_deal]
    )

    full1, qkv_dealt1, fc1_in1 = pin(full1, qkv_dealt1, fc1_in1)
    fc1_dealt1 = exchange(fc1_in1)
    qkv1 = join_qkv(qkv_dealt1)
    norm_attn1, norm_mlp1 = norms(full1, vectors[1])
    queries1, keys1, values1 = project(norm_attn1, qkv1, vectors[1])
    fc1_dealt1, push_in1, queries1, keys1 = pin(fc1_dealt1, push_in1, queries1, keys1)
    push_dealt1 = exchange(push_in1)
    attended1, probs1 = attend(queries1, keys1, values1)
    fc1_1 = join_fc1(fc1_dealt1)
    hidden1, slope1 = open_units(norm_mlp1, fc1_1, vectors[1])
    pushed1 = join_pushed(attended1, hidden1)
    push_back1 = push_blocks(pushed1, grad_full1)
    push_dealt1, push_back1, slope1, probs1 = pin(push_dealt1, push_back1, slope1, probs1)
    push_came1 = exchange(push_back1)
    push1 = join_push(push_dealt1)
    d_attended1, d_hidden1 = cut_pushed(dot_nt(grad_full1, push1))
    d_preact1 = (d_hidden1 * slope1).astype(BF16)
    fc1_back1 = fc1_blocks(norm_mlp1, d_preact1)
    d_scores1 = score_grads(values1, probs1, d_attended1)
    d_projected1 = attend_back(queries1, keys1, probs1, d_scores1, d_attended1)
    push_came1, fc1_back1, d_projected1 = pin(push_came1, fc1_back1, d_projected1)
    fc1_came1 = exchange(fc1_back1)
    d_scaled1, norm_sums1 = norm_grads(d_projected1, d_preact1, qkv1, fc1_1, full1, vectors[1])
    parts1 = plan.cut(d_scaled1)

    def pin_third(held):
        nonlocal fc1_came1
        fc1_came1, held = pin(fc1_came1, held)
        return held

    qkv_back1 = qkv_blocks(norm_attn1, d_projected1)
    last_parts = []

    def pin_push(came):
        nonlocal pushed1
        which = len(last_parts)
        part = dot_nn(plan.cut(pushed1)[which], push1).astype(BF16)
        part, pushed1, came = pin(part, pushed1, came)
        last_parts.append(part)
        return came

    grad_heads1, heads1 = plan.heads_of(grad_full1), plan.heads_of(full1)
    grad0, grad_full0 = plan.sum_and_spread(
        parts1,
        lambda which, summed: input_grad(grad_heads1[which], heads1[which], summed),
        [pin_third, pin_push, pin_push],
        [pin_push],
    )
    total1 = vector_sums(norm_sums1, d_projected1, d_preact1, grad1)

    grad_full0, qkv_back1, total1 = pin(grad_full0, qkv_back1, total1)
    qkv_came1 = exchange(qkv_back1)
    push_back0 = push_blocks(pushed0, grad_full0)
    push_back0, grad_full0, qkv_came1 = pin(push_back0, grad_full0, qkv_came1)
    push_came0 = exchange(push_back0)
    d_attended0, d_hidden0 = cut_pushed(dot_nt(grad_full0, push0))
    d_preact0 = (d_hidden0 * slope0).astype(BF16)
    fc1_back0 = fc1_blocks(norm_mlp0, d_preact0)
    d_scores0 = score_grads(values0, probs0, d_attended0)
    push_came0, fc1_back0, d_scores0, came = pin(
        push_came0, fc1_back0, d_scores0, plan.send_half(last_parts, 2)
    )
    last_parts = plan.add_half(last_parts, came)
    fc1_came0 = exchange(fc1_back0)
    d_projected0 = attend_back(queries0, keys0, probs0, d_scores0, d_attended0)
    qkv_back0 = qkv_blocks(norm_attn0, d_projected0)
    d_scaled0, norm_sums0 = norm_grads(d_projected0, d_preact0, qkv0, fc1_0, full0, vectors[0])
    fc1_came0, qkv_back0, d_scaled0, norm_sums0, push_came0, push_came1, came = pin(
        fc1_came0,
        qkv_back0,
        d_scaled0,
        norm_sums0,
        push_came0,
        push_came1,
        plan.send_half(last_parts, 1),
    )
    last_parts = plan.add_half(last_parts, came)
    total = jnp.stack([vector_sums(norm_sums0, d_projected0, d_preact0, grad0), total1])
    sums = [
        (axis, 1 << b)
        for axis in ("section", "context", "tensor")
        for b in range(int(math.log2(lax.axis_size(axis))))
    ]
    last_rows = last_home = None

    def pin_sum(came):
        nonlocal total, last_rows, last_home
        other = flip(total, *sums.pop(0))
        if last_rows is None:
            last_came, other, came = pin(plan.send_half(last_parts, 0), other, came)
            last_sum = [
                v[: v.shape[0] // 2].astype(F32) + w.astype(F32)
                for v, w in zip(last_parts, last_came)
            ]
            last_rows = add_branch(middle_rows, jnp.concatenate(last_sum, axis=0), vectors[1])
        elif last_home is None:
            last_home, other, came = pin(take_home(last_rows, 1), other, came)
        else:
            other, came = pin(other, came)
        total = total + other
        return came

    d_rows0 = plan.collect(plan.cut(d_scaled0), pins=[pin_sum] * len(plan.chunks))[0]
    d_input = input_grad(grad0, first_rows, d_rows0)
    qkv_back0, d_input, other, push_came0, push_came1, fc1_came0, fc1_came1 = pin(
        qkv_back0,
        d_input,
        flip(total, *sums.pop(0)),
        push_came0,
        push_came1,
        fc1_came0,
        fc1_came1,
    )
    total = total + other

    qkv_came0 = exchange(qkv_back0)
    first_home = take_home(d_input, 0)
    for spot in sums:
        total = total + flip(total, *spot)
    push_all = finish(push_came0, push_came1)
    fc1_all = finish(fc1_came0, fc1_came1)
    fc1_out = fc1_all.transpose(2, 1, 0, 3).reshape(depth, heads_here * units)
    out_out = push_all[:, :, :half_head].transpose(1, 0, 2, 3).reshape(heads_here * HD, depth)
    fc2_out = push_all[:, :, half_head:].transpose(1, 0, 2, 3).reshape(heads_here * units, depth)
    qkv_came0, last_home, fc1_out, out_out, fc2_out = pin(
        qkv_came0, last_home, fc1_out, out_out, fc2_out
    )
    result = jnp.where(section == 0, first_home, last_home)
    qkv_all = finish(qkv_came0, qkv_came1)
    qkv_out = (
        qkv_all.reshape(2, heads_here, depth, 3, half_head)
        .transpose(2, 3, 1, 0, 4)
        .reshape(depth, 3, heads_here * HD)
    )
    total = jnp.where(section == 0, total[0], total[1])
    return (
        result[None],
        qkv_out[None],
        out_out[None],
        fc1_out[None],
        fc2_out[None],
        total[: 2 * width].reshape(1, 2, width),
        total[2 * width : 4 * width].reshape(1, 2, width),
        total[5 * width : 8 * width].reshape(1, 3, width),
        total[8 * width :][None],
        jnp.broadcast_to(total[4 * width : 5 * width], (1, 2, width)),
    )


def solution(mesh):
    return jax.shard_map(
        per_device,
        mesh=mesh,
        in_specs=(
            P("section", None, ("context", "tensor"), None),
            P(None, "context"),
            P(),
            P("section", "context", None, "tensor"),
            P("section", "tensor", "context"),
            P("section", "context", "tensor"),
            P("section", "tensor", "context"),
            P("section", None, None),
            P("section", None, None),
            P("section", None, None),
            P("section", None),
            P("section", None, None),
        ),
        out_specs=(
            P("section", None, ("context", "tensor"), None),
            P("section", "context", None, "tensor"),
            P("section", "tensor", "context"),
            P("section", "context", "tensor"),
            P("section", "tensor", "context"),
            P("section", None, None),
            P("section", None, None),
            P("section", None, None),
            P("section", None),
            P("section", None, None),
        ),
        check_vma=False,
    )
```

```python
import math

import jax
import jax.numpy as jnp
import numpy as np
from jax import lax
from jax.sharding import PartitionSpec as P

HD = 256
ROT = 64

EPSILON = 1e-05
ROTARY_BASE = 10000.0
MASKED = -1e30

BF16 = jnp.bfloat16
F32 = jnp.float32


def locate(placed, lengths):
    seq_ends = jnp.cumsum(lengths)
    seq_starts = seq_ends - lengths
    segment = jnp.sum((placed[:, None] >= seq_ends[None, :]).astype(jnp.int32), axis=1)
    chosen = segment[:, None] == jnp.arange(lengths.shape[0], dtype=jnp.int32)[None, :]
    seq_begin = jnp.sum(jnp.where(chosen, seq_starts[None, :], 0), axis=1)
    return (segment, placed - seq_begin)


def normalize_parts(values):
    row_mean = jnp.mean(values, axis=-1, keepdims=True)
    centered = values - row_mean
    inv_std = lax.rsqrt(jnp.mean(centered * centered, axis=-1, keepdims=True) + EPSILON)
    return (centered * inv_std, inv_std)


def angles(position):
    half_rot = ROT // 2
    frequency = ROTARY_BASE ** (-(jnp.arange(half_rot, dtype=F32) * 2.0) / ROT)
    phase_angle = position.astype(F32)[:, None] * frequency[None, :]
    return (jnp.cos(phase_angle), jnp.sin(phase_angle))


def rotate_pairs(values, cosine, sine_part):
    half_rot = ROT // 2
    leading = values[:, :half_rot]
    second = values[:, half_rot:ROT]
    return jnp.concatenate(
        [
            leading * cosine - second * sine_part,
            second * cosine + leading * sine_part,
            values[:, ROT:],
        ],
        axis=-1,
    )


def dot_tn(left_side, right_side):
    return lax.dot_general(
        left_side, right_side, (((0,), (0,)), ((), ())), preferred_element_type=F32
    )


def dot_nt(left_side, right_side):
    return lax.dot_general(
        left_side, right_side, (((1,), (1,)), ((), ())), preferred_element_type=F32
    )


def dot_nn(left_side, right_side):
    return jnp.dot(left_side, right_side, preferred_element_type=F32)


def pin(*values):
    return lax.optimization_barrier(values)


def flip(value, axis, mask):
    count = lax.axis_size(axis)
    return lax.ppermute(value, axis, [(place, place ^ mask) for place in range(count)])


def trade(value):
    return flip(value, "section", 1)


class Plan:
    def __init__(self, micro_count, heads_here, part_rows):
        self.contexts = lax.axis_size("context")
        self.tensors = lax.axis_size("tensor")
        self.heads = heads_here
        self.span = self.contexts // micro_count
        self.shares = self.span // heads_here
        self.part_rows = part_rows
        self.section = lax.axis_index("section")
        self.context = lax.axis_index("context")
        self.tensor = lax.axis_index("tensor")
        self.micro = self.context // self.span
        self.share = (self.context % self.span) // heads_here
        self.head = self.context % heads_here
        bits = [("context", 1 << b) for b in range(int(math.log2(heads_here)))]
        bits += [("tensor", 1 << b) for b in range(int(math.log2(self.tensors)))]
        ways = len(bits)
        cuts = [8 * ((part_rows // 8 * k + ways - 1) // ways) for k in range(ways + 1)]
        self.chunks = [(cuts[k], cuts[k + 1] - cuts[k]) for k in range(ways)]
        self.orders = [bits[k:] + bits[:k] for k in range(ways)]
        self.partners = 1 << ways
        head_flip, tensor_flip, row = [], [], []
        for (start, rows), order in zip(self.chunks, self.orders):
            for block in range(self.partners):
                masks = {"context": 0, "tensor": 0}
                for place, (axis, mask) in enumerate(order):
                    if block >> place & 1:
                        masks[axis] |= mask
                head_flip += [masks["context"]] * rows
                tensor_flip += [masks["tensor"]] * rows
                row += list(range(start, start + rows))
        self.head_flip = np.array(head_flip, np.int32)
        self.tensor_flip = np.array(tensor_flip, np.int32)
        self.row = np.array(row, np.int32)
        self.rows = len(row)

    def cut(self, full):
        return [
            full[start * self.partners : (start + rows) * self.partners]
            for start, rows in self.chunks
        ]

    def spread(self, *owns, pins=()):
        held = [own[start : start + rows] for own in owns for start, rows in self.chunks]
        orders = self.orders * len(owns)
        steps = len(self.chunks)
        for step in range(steps):
            came = [flip(v, *order[step]) for v, order in zip(held, orders)]
            came = list(pins[step](came) if step < len(pins) else pin(*came))
            if step < steps - 1:
                held = [jnp.concatenate([v, w], axis=0) for v, w in zip(held, came)]
                held = list(pin(*held))
        pairs = [v for pair in zip(held, came) for v in pair]
        each = len(pairs) // len(owns)
        return [jnp.concatenate(pairs[k : k + each], axis=0) for k in range(0, len(pairs), each)]

    def collect(self, *sets, pins=()):
        held = [part for parts in sets for part in parts]
        orders = self.orders * len(sets)
        steps = len(self.chunks)
        for count, step in enumerate(reversed(range(steps))):
            came = [flip(v[v.shape[0] // 2 :], *order[step]) for v, order in zip(held, orders)]
            came = list(pins[count](came) if count < len(pins) else pin(*came))
            held = [v[: v.shape[0] // 2].astype(F32) + w.astype(F32) for v, w in zip(held, came)]
            if step:
                held = list(pin(*[v.astype(BF16) for v in held]))
        return [jnp.concatenate(held[k : k + steps], axis=0) for k in range(0, len(held), steps)]

    def heads_of(self, full):
        return [
            full[start * self.partners : start * self.partners + 2 * rows]
            for start, rows in self.chunks
        ]

    def own_of(self, pairs):
        return jnp.concatenate([v[: v.shape[0] // 2] for v in pairs], axis=0)

    def sum_and_spread(self, parts, mix, sum_pins=(), spread_pins=()):
        steps = len(self.chunks)
        held = list(parts)
        for count, step in enumerate(range(steps - 1, 0, -1)):
            came = self.send_half(held, step)
            came = list(sum_pins[count](came) if count < len(sum_pins) else pin(*came))
            held = list(pin(*self.add_half(held, came)))
        came = self.send(held, 0)
        came = list(sum_pins[steps - 1](came) if len(sum_pins) >= steps else pin(*came))
        pairs = []
        for which, (v, w) in enumerate(zip(held, came)):
            half = v.shape[0] // 2
            swapped = jnp.concatenate([w[half:], w[:half]], axis=0)
            pairs.append(mix(which, v.astype(F32) + swapped.astype(F32)))
        pairs = list(pin(*pairs))
        held = pairs
        for count, step in enumerate(range(1, steps)):
            came = self.send(held, step)
            came = list(spread_pins[count](came) if count < len(spread_pins) else pin(*came))
            if step < steps - 1:
                held = list(pin(*self.join(held, came)))
        return self.own_of(pairs), self.whole(held, came)

    def pieces(self, own):
        return [own[start : start + rows] for start, rows in self.chunks]

    def send(self, held, step):
        return [flip(v, *order[step]) for v, order in zip(held, self.orders)]

    def join(self, held, came):
        return [jnp.concatenate([v, w], axis=0) for v, w in zip(held, came)]

    def whole(self, held, came):
        return jnp.concatenate([v for pair in zip(held, came) for v in pair], axis=0)

    def send_half(self, held, step):
        return [flip(v[v.shape[0] // 2 :], *order[step]) for v, order in zip(held, self.orders)]

    def add_half(self, held, came):
        return [
            (v[: v.shape[0] // 2].astype(F32) + w.astype(F32)).astype(BF16)
            for v, w in zip(held, came)
        ]

    def rows_of(self, places, section, share):
        context = section * self.span + share * self.heads + (self.head ^ self.head_flip)
        chosen = context[:, None] == jnp.arange(self.contexts, dtype=jnp.int32)[None, :]
        first = jnp.sum(jnp.where(chosen, places[None, :], 0), axis=1)
        within = (self.tensor ^ self.tensor_flip) * self.part_rows + self.row
        return first + within * self.contexts


def per_device(
    boundary,
    token_places,
    lengths,
    qkv_weight,
    out_weight,
    fc1_weight,
    fc2_weight,
    norm_gain,
    norm_bias,
    qkv_bias,
    fc1_bias,
    branch_bias,
):
    micro_count, part_rows, width = boundary.shape[1:]
    depth = qkv_weight.shape[1]
    heads_here = qkv_weight.shape[3] // HD
    units = fc1_weight.shape[2] // heads_here
    all_units = fc1_bias.shape[1]
    plan = Plan(micro_count, heads_here, part_rows)
    section, span, contexts = plan.section, plan.span, plan.contexts
    half_head, half_units = HD // 2, units // 2
    half_push = half_head + half_units
    copies = micro_count * plan.shares
    score_scale = 1.0 / math.sqrt(HD)
    head_index = plan.tensor * heads_here + plan.head

    def in_order(own, other):
        return (jnp.where(section == 0, own, other), jnp.where(section == 0, other, own))

    def flat(place_section, place_context):
        return place_section * contexts + place_context

    def bring(origin, held):
        came = []
        for micro in range(micro_count):
            pairs = [
                (flat(origin, side * span + k), flat(side, micro * span + k))
                for side in range(micro_count)
                for k in range(span)
            ]
            came.append(lax.ppermute(held[micro], ("section", "context"), pairs))
        return jnp.where(plan.micro == 0, came[0], came[1])

    def take_home(own, target):
        came = []
        for micro in range(micro_count):
            pairs = [
                (flat(side, micro * span + k), flat(target, side * span + k))
                for side in range(micro_count)
                for k in range(span)
            ]
            came.append(lax.ppermute(own, ("section", "context"), pairs))
        return jnp.stack(came)

    def half_of(halves):
        kept = lax.dynamic_index_in_dim(halves, section, 0, keepdims=False)
        return kept, trade(lax.dynamic_index_in_dim(halves, 1 - section, 0, keepdims=False))

    def exchange(blocks):
        return lax.all_to_all(blocks, "context", split_axis=0, concat_axis=0, tiled=True)

    def repeat(half, layer):
        blocks = in_order(*half)[layer]
        spread = jnp.broadcast_to(blocks[None], (copies,) + blocks.shape)
        return spread.reshape((contexts,) + blocks.shape[1:])

    def split_qkv():
        blocks = qkv_weight[0].reshape(depth, 3, heads_here, 2, half_head)
        return half_of(blocks.transpose(3, 2, 0, 1, 4).reshape(2, heads_here, depth, 3 * half_head))

    def split_fc1():
        blocks = fc1_weight[0].reshape(depth, heads_here, 2, half_units)
        return half_of(blocks.transpose(2, 1, 0, 3))

    def split_push():
        blocks = jnp.concatenate(
            [
                out_weight[0].reshape(heads_here, 2, half_head, depth),
                fc2_weight[0].reshape(heads_here, 2, half_units, depth),
            ],
            axis=2,
        )
        return half_of(blocks.transpose(1, 0, 2, 3))

    def join_qkv(dealt):
        own = dealt.reshape(width, 3, half_head)
        low, high = in_order(own, trade(own))
        return jnp.stack([low, high], axis=2).reshape(width, 3 * HD)

    def join_fc1(dealt):
        own = dealt.reshape(width, half_units)
        return jnp.concatenate([own, trade(own)], axis=1)

    def join_push(dealt):
        own = dealt.transpose(1, 0, 2).reshape(half_push, width)
        return jnp.concatenate([own, trade(own)], axis=0)

    def gather_places():
        first = lax.all_gather(token_places[:, 0], "context", axis=0)
        return lax.dynamic_index_in_dim(first, plan.micro, 1, keepdims=False)

    def find_places(places):
        own_lengths = lax.dynamic_index_in_dim(lengths, plan.micro, 0, keepdims=False)
        own_spot = locate(plan.rows_of(places, section, plan.share), own_lengths)
        key_spots = [
            locate(plan.rows_of(places, section ^ side, plan.share ^ share), own_lengths)
            for side in range(2)
            for share in range(plan.shares)
        ]
        return own_spot, [jnp.concatenate(part) for part in zip(*key_spots)]

    def share_keys(value):
        held = [value]
        for share in range(1, plan.shares):
            held.append(flip(value, "context", share * heads_here))
        pile = jnp.concatenate(held, axis=0)
        return jnp.concatenate([pile, trade(pile)], axis=0)

    def return_keys(value):
        half = value.shape[0] // 2
        pile = value[:half] + trade(value[half:].astype(BF16)).astype(F32)
        total = pile[: plan.rows]
        for share in range(1, plan.shares):
            piece = pile[share * plan.rows : (share + 1) * plan.rows].astype(BF16)
            total = total + flip(piece, "context", share * heads_here).astype(F32)
        return total

    own_vector = jnp.concatenate(
        [
            norm_gain[0].reshape(-1),
            norm_bias[0].reshape(-1),
            branch_bias[0, 0] + branch_bias[0, 1],
            lax.dynamic_slice(qkv_bias[0], (0, head_index * HD), (3, HD)).reshape(-1),
            lax.dynamic_slice_in_dim(fc1_bias[0], head_index * units, units),
        ]
    )

    def unit_order(values):
        first, second = in_order(values[..., :half_units], values[..., half_units:])
        return jnp.concatenate([first, second], axis=-1)

    def cut_vector(vector):
        gain = vector[: 2 * width].reshape(2, width)
        bias = vector[2 * width : 4 * width].reshape(2, width)
        out_shift = vector[4 * width : 5 * width]
        qkv_shift = vector[5 * width : 5 * width + 3 * HD]
        return gain, bias, out_shift, qkv_shift, unit_order(vector[5 * width + 3 * HD :])

    def scaled_rows(full_rows):
        return normalize_parts(full_rows.astype(F32))[0]

    def norms(full_rows, vectors):
        gain, bias = vectors[:2]
        scaled = scaled_rows(full_rows)
        return [(scaled * gain[k] + bias[k]).astype(BF16) for k in range(2)]

    def project(norm_attn, qkv_full, vectors):
        projected = dot_nn(norm_attn, qkv_full) + vectors[3]
        queries = rotate_pairs(projected[:, :HD], cosine, sine_part).astype(BF16)
        key_rows = rotate_pairs(projected[:, HD : 2 * HD], cosine, sine_part).astype(BF16)
        value_rows = projected[:, 2 * HD :].astype(BF16)
        key_value = share_keys(jnp.concatenate([key_rows, value_rows], axis=1))
        return queries, key_value[:, :HD], key_value[:, HD:]

    def attend(queries, keys, values):
        scores = dot_nt(queries, keys) * score_scale
        masked = jnp.where(allowed, scores, MASKED)
        top = jnp.max(masked, axis=1, keepdims=True)
        weight = jnp.where(allowed, jnp.exp(masked - top), 0.0)
        probs = weight / jnp.sum(weight, axis=1, keepdims=True)
        return dot_nn(probs.astype(BF16), values).astype(BF16), probs

    def score_grads(values, probs, d_attended):
        d_probs = dot_nt(d_attended, values)
        centre = jnp.sum(probs * d_probs, axis=1, keepdims=True)
        return (probs * (d_probs - centre)).astype(BF16)

    def head_grads(queries, keys, probs, d_scores, d_attended):
        d_queries = dot_nn(d_scores, keys) * score_scale
        d_keys = dot_tn(d_scores, queries) * score_scale
        d_values = dot_tn(probs.astype(BF16), d_attended)
        return d_queries, jnp.concatenate([d_keys, d_values], axis=1)

    def turn_back(d_queries, d_key_values):
        key_grads = return_keys(d_key_values)
        return jnp.concatenate(
            [
                rotate_pairs(d_queries, cosine, -sine_part),
                rotate_pairs(key_grads[:, :HD], cosine, -sine_part),
                key_grads[:, HD:],
            ],
            axis=1,
        ).astype(BF16)

    def join_pushed(attended, hidden):
        first, second = in_order(attended[:, :half_head], attended[:, half_head:])
        return jnp.concatenate(
            [first, hidden[:, :half_units], second, hidden[:, half_units:]], axis=1
        )

    def cut_pushed(d_pushed):
        first, second = in_order(
            d_pushed[:, :half_head], d_pushed[:, half_push : half_push + half_head]
        )
        d_attended = jnp.concatenate([first, second], axis=1).astype(BF16)
        d_hidden = jnp.concatenate(
            [d_pushed[:, half_head:half_push], d_pushed[:, half_push + half_head :]], axis=1
        )
        return d_attended, d_hidden

    def push(pushed, push_full):
        return [dot_nn(rows, push_full).astype(BF16) for rows in plan.cut(pushed)]

    def add_branch(own_rows, summed, vectors):
        return (own_rows.astype(F32) + summed + vectors[2]).astype(BF16)

    def sum_cores(rows, own, other):
        came = trade(dot_tn(rows, other).astype(BF16))
        return (dot_tn(rows, own) + came.astype(F32)).astype(BF16)

    def push_blocks(pushed, grad_full):
        came = trade(dot_tn(pushed[:, half_push:], grad_full).astype(BF16))
        half = (dot_tn(pushed[:, :half_push], grad_full) + came.astype(F32)).astype(BF16)
        return half.reshape(half_push, contexts, depth).transpose(1, 0, 2)

    def fc1_blocks(norm_mlp, d_preact):
        half = sum_cores(norm_mlp, d_preact[:, :half_units], d_preact[:, half_units:])
        return half.reshape(contexts, depth, half_units)

    def qkv_blocks(norm_attn, d_projected):
        parts = d_projected.reshape(plan.rows, 3, 2, half_head)
        own, other = in_order(parts[:, :, 0], parts[:, :, 1])
        shape = (plan.rows, 3 * half_head)
        half = sum_cores(norm_attn, own.reshape(shape), other.reshape(shape))
        return half.reshape(contexts, depth, 3 * half_head)

    def gather_sum(came):
        return jnp.sum(came.reshape((copies, heads_here) + came.shape[1:]).astype(F32), axis=0)

    def norm_grads(d_projected, d_preact, qkv_full, fc1_full, full_rows, vectors, pin=None):
        d_norm_attn = dot_nt(d_projected, qkv_full)
        if pin is not None:
            d_norm_attn, d_preact = pin(d_norm_attn, d_preact)
        d_norm_mlp = dot_nt(d_preact, fc1_full)
        gain = vectors[0]
        d_scaled = (d_norm_attn * gain[0] + d_norm_mlp * gain[1]).astype(BF16)
        scaled = scaled_rows(full_rows)
        sums = [
            jnp.sum(d_norm_attn * scaled, axis=0),
            jnp.sum(d_norm_mlp * scaled, axis=0),
            jnp.sum(d_norm_attn, axis=0),
            jnp.sum(d_norm_mlp, axis=0),
        ]
        return d_scaled, sums

    def input_grad(grad_own, own_rows, d_scaled):
        own_scaled, own_inv = normalize_parts(own_rows.astype(F32))
        d_input = grad_own.astype(F32) + own_inv * (
            d_scaled
            - jnp.mean(d_scaled, axis=-1, keepdims=True)
            - own_scaled * jnp.mean(d_scaled * own_scaled, axis=-1, keepdims=True)
        )
        return d_input.astype(BF16)

    def vector_sums(norm_sums, d_projected, d_preact, grad_own):
        qkv_part = lax.dynamic_update_slice(
            jnp.zeros((3, width), F32),
            jnp.sum(d_projected, axis=0, dtype=F32).reshape(3, HD),
            (0, head_index * HD),
        )
        unit_part = lax.dynamic_update_slice_in_dim(
            jnp.zeros((all_units,), F32),
            unit_order(jnp.sum(d_preact, axis=0, dtype=F32)),
            head_index * units,
            0,
        )
        return jnp.concatenate(
            norm_sums
            + [jnp.sum(grad_own.astype(F32), axis=0), qkv_part.reshape(-1), unit_part]
        )

    def open_units(norm_mlp, fc1_full, vectors):
        preact = dot_nn(norm_mlp, fc1_full) + vectors[4]
        below = 0.5 * (1.0 + lax.erf(preact * math.sqrt(0.5)))
        bell = jnp.exp(-0.5 * preact * preact) * (1.0 / math.sqrt(2.0 * math.pi))
        return (preact * below).astype(BF16), below + preact * bell

    def finish(came0, came1):
        mine, yours = in_order(gather_sum(came0), gather_sum(came1))
        return jnp.stack(in_order(mine, trade(yours.astype(BF16)).astype(F32)))

    rows_in = [boundary[0, k] for k in range(micro_count)]
    first_rows = bring(0, rows_in)
    first_rows, qkv_weight, places, own_vector = pin(
        first_rows, qkv_weight, gather_places(), own_vector
    )
    qkv_half = split_qkv()

    def pin_gather(came):
        nonlocal qkv_half, own_vector, rows_in
        qkv_half, own_vector, rows_in, came = pin(qkv_half, own_vector, rows_in, came)
        return came

    full0 = plan.spread(first_rows, pins=[pin_gather])[0]
    qkv_in0 = repeat(qkv_half, 0)
    other_vector = trade(own_vector)
    grad1 = bring(1, rows_in)
    full0, qkv_in0, grad1, other_vector, fc1_weight, out_weight, fc2_weight = pin(
        full0, qkv_in0, grad1, other_vector, fc1_weight, out_weight, fc2_weight
    )
    (segment, position), (seg_keys, pos_keys) = find_places(places)
    fc1_half = split_fc1()
    fc1_in0 = repeat(fc1_half, 0)
    held1 = plan.pieces(grad1)
    vectors = [cut_vector(vector) for vector in in_order(own_vector, other_vector)]

    qkv_dealt0 = exchange(qkv_in0)
    norm_attn0, norm_mlp0 = norms(full0, vectors[0])
    push_half = split_push()
    qkv_dealt0, fc1_in0, push_half, norm_attn0, norm_mlp0, came1 = pin(
        qkv_dealt0, fc1_in0, push_half, norm_attn0, norm_mlp0, plan.send(held1, 0)
    )
    held1 = plan.join(held1, came1)
    fc1_dealt0 = exchange(fc1_in0)
    allowed = (segment[:, None] == seg_keys[None, :]) & (pos_keys[None, :] <= position[:, None])
    cosine, sine_part = angles(position)
    qkv0 = join_qkv(qkv_dealt0)
    queries0, keys0, values0 = project(norm_attn0, qkv0, vectors[0])
    push_in0 = repeat(push_half, 0)
    fc1_dealt0, push_in0, queries0, keys0, came1 = pin(
        fc1_dealt0, push_in0, queries0, keys0, plan.send(held1, 1)
    )
    held1 = plan.join(held1, came1)
    push_dealt0 = exchange(push_in0)
    attended0, probs0 = attend(queries0, keys0, values0)
    fc1_0 = join_fc1(fc1_dealt0)
    hidden0, slope0 = open_units(norm_mlp0, fc1_0, vectors[0])
    pushed0 = join_pushed(attended0, hidden0)
    qkv_in1, fc1_in1, push_in1 = [repeat(half, 1) for half in (qkv_half, fc1_half, push_half)]
    pushed0, probs0, slope0, push_dealt0, qkv_in1, fc1_in1, push_in1, came1 = pin(
        pushed0, probs0, slope0, push_dealt0, qkv_in1, fc1_in1, push_in1, plan.send(held1, 2)
    )
    grad_full1 = plan.whole(held1, came1)
    qkv_dealt1 = exchange(qkv_in1)
    push0 = join_push(push_dealt0)
    parts0 = push(pushed0, push0)

    def pin_deal(came):
        nonlocal qkv_dealt1
        qkv_dealt1, came = pin(qkv_dealt1, came)
        return came

    heads0 = plan.heads_of(full0)
    middle_rows, full1 = plan.sum_and_spread(
        parts0, lambda which, summed: add_branch(heads0[which], summed, vectors[0]), [pin_deal]
    )

    full1, qkv_dealt1, fc1_in1 = pin(full1, qkv_dealt1, fc1_in1)
    fc1_dealt1 = exchange(fc1_in1)
    qkv1 = join_qkv(qkv_dealt1)
    norm_attn1, norm_mlp1 = norms(full1, vectors[1])
    queries1, keys1, values1 = project(norm_attn1, qkv1, vectors[1])
    fc1_dealt1, push_in1, queries1, keys1 = pin(fc1_dealt1, push_in1, queries1, keys1)
    push_dealt1 = exchange(push_in1)
    attended1, probs1 = attend(queries1, keys1, values1)
    fc1_1 = join_fc1(fc1_dealt1)
    hidden1, slope1 = open_units(norm_mlp1, fc1_1, vectors[1])
    pushed1 = join_pushed(attended1, hidden1)
    push_back1 = push_blocks(pushed1, grad_full1)
    push_dealt1, push_back1, slope1, probs1 = pin(push_dealt1, push_back1, slope1, probs1)
    push_came1 = exchange(push_back1)
    push1 = join_push(push_dealt1)
    d_attended1, d_hidden1 = cut_pushed(dot_nt(grad_full1, push1))
    d_preact1 = (d_hidden1 * slope1).astype(BF16)
    fc1_back1 = fc1_blocks(norm_mlp1, d_preact1)
    d_scores1 = score_grads(values1, probs1, d_attended1)
    d_projected1 = turn_back(*head_grads(queries1, keys1, probs1, d_scores1, d_attended1))
    push_came1, fc1_back1, d_projected1 = pin(push_came1, fc1_back1, d_projected1)
    fc1_came1 = exchange(fc1_back1)
    d_scaled1, norm_sums1 = norm_grads(d_projected1, d_preact1, qkv1, fc1_1, full1, vectors[1])
    parts1 = plan.cut(d_scaled1)

    def pin_third(held):
        nonlocal fc1_came1
        fc1_came1, held = pin(fc1_came1, held)
        return held

    qkv_back1 = qkv_blocks(norm_attn1, d_projected1)
    last_parts = []

    def pin_push(came):
        nonlocal pushed1
        which = len(last_parts)
        part = dot_nn(plan.cut(pushed1)[which], push1).astype(BF16)
        part, pushed1, came = pin(part, pushed1, came)
        last_parts.append(part)
        return came

    grad_heads1, heads1 = plan.heads_of(grad_full1), plan.heads_of(full1)
    grad0, grad_full0 = plan.sum_and_spread(
        parts1,
        lambda which, summed: input_grad(grad_heads1[which], heads1[which], summed),
        [pin_third, pin_push, pin_push],
        [pin_push],
    )
    total1 = vector_sums(norm_sums1, d_projected1, d_preact1, grad1)

    grad_full0, qkv_back1, total1 = pin(grad_full0, qkv_back1, total1)
    qkv_came1 = exchange(qkv_back1)
    push_back0 = push_blocks(pushed0, grad_full0)
    push_back0, grad_full0, qkv_came1 = pin(push_back0, grad_full0, qkv_came1)
    push_came0 = exchange(push_back0)
    d_attended0, d_hidden0 = cut_pushed(dot_nt(grad_full0, push0))
    d_preact0 = (d_hidden0 * slope0).astype(BF16)
    fc1_back0 = fc1_blocks(norm_mlp0, d_preact0)
    d_scores0 = score_grads(values0, probs0, d_attended0)
    head_grads0 = head_grads(queries0, keys0, probs0, d_scores0, d_attended0)
    push_came0, fc1_back0, head_grads0, came = pin(
        push_came0, fc1_back0, head_grads0, plan.send_half(last_parts, 2)
    )
    fc1_came0 = exchange(fc1_back0)
    d_projected0 = turn_back(*head_grads0)
    d_projected0, last_parts, came = pin(d_projected0, last_parts, came)
    last_parts = plan.add_half(last_parts, came)
    qkv_back0 = qkv_blocks(norm_attn0, d_projected0)
    d_scaled0, norm_sums0 = norm_grads(d_projected0, d_preact0, qkv0, fc1_0, full0, vectors[0])
    fc1_came0, qkv_back0, d_scaled0, norm_sums0, push_came0, push_came1, came = pin(
        fc1_came0,
        qkv_back0,
        d_scaled0,
        norm_sums0,
        push_came0,
        push_came1,
        plan.send_half(last_parts, 1),
    )
    last_parts = plan.add_half(last_parts, came)
    total = jnp.stack([vector_sums(norm_sums0, d_projected0, d_preact0, grad0), total1])
    sums = [
        (axis, 1 << b)
        for axis in ("section", "context", "tensor")
        for b in range(int(math.log2(lax.axis_size(axis))))
    ]
    last_rows = last_home = None

    def pin_sum(came):
        nonlocal total, last_rows, last_home
        other = flip(total, *sums.pop(0))
        if last_rows is None:
            last_came, other, came = pin(plan.send_half(last_parts, 0), other, came)
            last_sum = [
                v[: v.shape[0] // 2].astype(F32) + w.astype(F32)
                for v, w in zip(last_parts, last_came)
            ]
            last_rows = add_branch(middle_rows, jnp.concatenate(last_sum, axis=0), vectors[1])
        elif last_home is None:
            last_home, other, came = pin(take_home(last_rows, 1), other, came)
        else:
            other, came = pin(other, came)
        total = total + other
        return came

    d_rows0 = plan.collect(plan.cut(d_scaled0), pins=[pin_sum] * len(plan.chunks))[0]
    d_input = input_grad(grad0, first_rows, d_rows0)
    qkv_back0, d_input, other, push_came0, push_came1, fc1_came0, fc1_came1 = pin(
        qkv_back0,
        d_input,
        flip(total, *sums.pop(0)),
        push_came0,
        push_came1,
        fc1_came0,
        fc1_came1,
    )
    total = total + other

    qkv_came0 = exchange(qkv_back0)
    first_home = take_home(d_input, 0)
    for spot in sums:
        total = total + flip(total, *spot)
    push_all = finish(push_came0, push_came1)
    fc1_all = finish(fc1_came0, fc1_came1)
    fc1_out = fc1_all.transpose(2, 1, 0, 3).reshape(depth, heads_here * units)
    out_out = push_all[:, :, :half_head].transpose(1, 0, 2, 3).reshape(heads_here * HD, depth)
    fc2_out = push_all[:, :, half_head:].transpose(1, 0, 2, 3).reshape(heads_here * units, depth)
    qkv_came0, last_home, fc1_out, out_out, fc2_out = pin(
        qkv_came0, last_home, fc1_out, out_out, fc2_out
    )
    result = jnp.where(section == 0, first_home, last_home)
    qkv_all = finish(qkv_came0, qkv_came1)
    qkv_out = (
        qkv_all.reshape(2, heads_here, depth, 3, half_head)
        .transpose(2, 3, 1, 0, 4)
        .reshape(depth, 3, heads_here * HD)
    )
    total = jnp.where(section == 0, total[0], total[1])
    return (
        result[None],
        qkv_out[None],
        out_out[None],
        fc1_out[None],
        fc2_out[None],
        total[: 2 * width].reshape(1, 2, width),
        total[2 * width : 4 * width].reshape(1, 2, width),
        total[5 * width : 8 * width].reshape(1, 3, width),
        total[8 * width :][None],
        jnp.broadcast_to(total[4 * width : 5 * width], (1, 2, width)),
    )


def solution(mesh):
    return jax.shard_map(
        per_device,
        mesh=mesh,
        in_specs=(
            P("section", None, ("context", "tensor"), None),
            P(None, "context"),
            P(),
            P("section", "context", None, "tensor"),
            P("section", "tensor", "context"),
            P("section", "context", "tensor"),
            P("section", "tensor", "context"),
            P("section", None, None),
            P("section", None, None),
            P("section", None, None),
            P("section", None),
            P("section", None, None),
        ),
        out_specs=(
            P("section", None, ("context", "tensor"), None),
            P("section", "context", None, "tensor"),
            P("section", "tensor", "context"),
            P("section", "context", "tensor"),
            P("section", "tensor", "context"),
            P("section", None, None),
            P("section", None, None),
            P("section", None, None),
            P("section", None),
            P("section", None, None),
        ),
        check_vma=False,
    )
```

```python
import math

import jax
import jax.numpy as jnp
import numpy as np
from jax import lax
from jax.sharding import PartitionSpec as P

HD = 256
ROT = 64

EPSILON = 1e-05
ROTARY_BASE = 10000.0
MASKED = -1e30

BF16 = jnp.bfloat16
F32 = jnp.float32


def locate(placed, lengths):
    seq_ends = jnp.cumsum(lengths)
    seq_starts = seq_ends - lengths
    segment = jnp.sum((placed[:, None] >= seq_ends[None, :]).astype(jnp.int32), axis=1)
    chosen = segment[:, None] == jnp.arange(lengths.shape[0], dtype=jnp.int32)[None, :]
    seq_begin = jnp.sum(jnp.where(chosen, seq_starts[None, :], 0), axis=1)
    return (segment, placed - seq_begin)


def normalize_parts(values):
    row_mean = jnp.mean(values, axis=-1, keepdims=True)
    centered = values - row_mean
    inv_std = lax.rsqrt(jnp.mean(centered * centered, axis=-1, keepdims=True) + EPSILON)
    return (centered * inv_std, inv_std)


def angles(position):
    half_rot = ROT // 2
    frequency = ROTARY_BASE ** (-(jnp.arange(half_rot, dtype=F32) * 2.0) / ROT)
    phase_angle = position.astype(F32)[:, None] * frequency[None, :]
    return (jnp.cos(phase_angle), jnp.sin(phase_angle))


def rotate_pairs(values, cosine, sine_part):
    half_rot = ROT // 2
    leading = values[:, :half_rot]
    second = values[:, half_rot:ROT]
    return jnp.concatenate(
        [
            leading * cosine - second * sine_part,
            second * cosine + leading * sine_part,
            values[:, ROT:],
        ],
        axis=-1,
    )


def dot_tn(left_side, right_side):
    return lax.dot_general(
        left_side, right_side, (((0,), (0,)), ((), ())), preferred_element_type=F32
    )


def dot_nt(left_side, right_side):
    return lax.dot_general(
        left_side, right_side, (((1,), (1,)), ((), ())), preferred_element_type=F32
    )


def dot_nn(left_side, right_side):
    return jnp.dot(left_side, right_side, preferred_element_type=F32)


def pin(*values):
    return lax.optimization_barrier(values)


def flip(value, axis, mask):
    count = lax.axis_size(axis)
    return lax.ppermute(value, axis, [(place, place ^ mask) for place in range(count)])


def trade(value):
    return flip(value, "section", 1)


class Plan:
    def __init__(self, micro_count, heads_here, part_rows):
        self.contexts = lax.axis_size("context")
        self.tensors = lax.axis_size("tensor")
        self.heads = heads_here
        self.span = self.contexts // micro_count
        self.shares = self.span // heads_here
        self.part_rows = part_rows
        self.section = lax.axis_index("section")
        self.context = lax.axis_index("context")
        self.tensor = lax.axis_index("tensor")
        self.micro = self.context // self.span
        self.share = (self.context % self.span) // heads_here
        self.head = self.context % heads_here
        bits = [("context", 1 << b) for b in range(int(math.log2(heads_here)))]
        bits += [("tensor", 1 << b) for b in range(int(math.log2(self.tensors)))]
        ways = len(bits)
        cuts = [8 * ((part_rows // 8 * k + ways - 1) // ways) for k in range(ways + 1)]
        self.chunks = [(cuts[k], cuts[k + 1] - cuts[k]) for k in range(ways)]
        self.orders = [bits[k:] + bits[:k] for k in range(ways)]
        self.partners = 1 << ways
        head_flip, tensor_flip, row = [], [], []
        for (start, rows), order in zip(self.chunks, self.orders):
            for block in range(self.partners):
                masks = {"context": 0, "tensor": 0}
                for place, (axis, mask) in enumerate(order):
                    if block >> place & 1:
                        masks[axis] |= mask
                head_flip += [masks["context"]] * rows
                tensor_flip += [masks["tensor"]] * rows
                row += list(range(start, start + rows))
        self.head_flip = np.array(head_flip, np.int32)
        self.tensor_flip = np.array(tensor_flip, np.int32)
        self.row = np.array(row, np.int32)
        self.rows = len(row)

    def cut(self, full):
        return [
            full[start * self.partners : (start + rows) * self.partners]
            for start, rows in self.chunks
        ]

    def spread(self, *owns, pins=()):
        held = [own[start : start + rows] for own in owns for start, rows in self.chunks]
        orders = self.orders * len(owns)
        steps = len(self.chunks)
        for step in range(steps):
            came = [flip(v, *order[step]) for v, order in zip(held, orders)]
            came = list(pins[step](came) if step < len(pins) else pin(*came))
            if step < steps - 1:
                held = [jnp.concatenate([v, w], axis=0) for v, w in zip(held, came)]
                held = list(pin(*held))
        pairs = [v for pair in zip(held, came) for v in pair]
        each = len(pairs) // len(owns)
        return [jnp.concatenate(pairs[k : k + each], axis=0) for k in range(0, len(pairs), each)]

    def collect(self, *sets, pins=()):
        held = [part for parts in sets for part in parts]
        orders = self.orders * len(sets)
        steps = len(self.chunks)
        for count, step in enumerate(reversed(range(steps))):
            came = [flip(v[v.shape[0] // 2 :], *order[step]) for v, order in zip(held, orders)]
            came = list(pins[count](came) if count < len(pins) else pin(*came))
            held = [v[: v.shape[0] // 2].astype(F32) + w.astype(F32) for v, w in zip(held, came)]
            if step:
                held = list(pin(*[v.astype(BF16) for v in held]))
        return [jnp.concatenate(held[k : k + steps], axis=0) for k in range(0, len(held), steps)]

    def heads_of(self, full):
        return [
            full[start * self.partners : start * self.partners + 2 * rows]
            for start, rows in self.chunks
        ]

    def own_of(self, pairs):
        return jnp.concatenate([v[: v.shape[0] // 2] for v in pairs], axis=0)

    def sum_and_spread(self, parts, mix, sum_pins=(), spread_pins=()):
        steps = len(self.chunks)
        held = list(parts)
        for count, step in enumerate(range(steps - 1, 0, -1)):
            came = self.send_half(held, step)
            came = list(sum_pins[count](came) if count < len(sum_pins) else pin(*came))
            held = list(pin(*self.add_half(held, came)))
        came = self.send(held, 0)
        came = list(sum_pins[steps - 1](came) if len(sum_pins) >= steps else pin(*came))
        pairs = []
        for which, (v, w) in enumerate(zip(held, came)):
            half = v.shape[0] // 2
            swapped = jnp.concatenate([w[half:], w[:half]], axis=0)
            pairs.append(mix(which, v.astype(F32) + swapped.astype(F32)))
        pairs = list(pin(*pairs))
        held = pairs
        for count, step in enumerate(range(1, steps)):
            came = self.send(held, step)
            came = list(spread_pins[count](came) if count < len(spread_pins) else pin(*came))
            if step < steps - 1:
                held = list(pin(*self.join(held, came)))
        return self.own_of(pairs), self.whole(held, came)

    def pieces(self, own):
        return [own[start : start + rows] for start, rows in self.chunks]

    def send(self, held, step):
        return [flip(v, *order[step]) for v, order in zip(held, self.orders)]

    def join(self, held, came):
        return [jnp.concatenate([v, w], axis=0) for v, w in zip(held, came)]

    def whole(self, held, came):
        return jnp.concatenate([v for pair in zip(held, came) for v in pair], axis=0)

    def send_half(self, held, step):
        return [flip(v[v.shape[0] // 2 :], *order[step]) for v, order in zip(held, self.orders)]

    def add_half(self, held, came):
        return [
            (v[: v.shape[0] // 2].astype(F32) + w.astype(F32)).astype(BF16)
            for v, w in zip(held, came)
        ]

    def rows_of(self, places, section, share):
        context = section * self.span + share * self.heads + (self.head ^ self.head_flip)
        chosen = context[:, None] == jnp.arange(self.contexts, dtype=jnp.int32)[None, :]
        first = jnp.sum(jnp.where(chosen, places[None, :], 0), axis=1)
        within = (self.tensor ^ self.tensor_flip) * self.part_rows + self.row
        return first + within * self.contexts


def per_device(
    boundary,
    token_places,
    lengths,
    qkv_weight,
    out_weight,
    fc1_weight,
    fc2_weight,
    norm_gain,
    norm_bias,
    qkv_bias,
    fc1_bias,
    branch_bias,
):
    micro_count, part_rows, width = boundary.shape[1:]
    depth = qkv_weight.shape[1]
    heads_here = qkv_weight.shape[3] // HD
    units = fc1_weight.shape[2] // heads_here
    all_units = fc1_bias.shape[1]
    plan = Plan(micro_count, heads_here, part_rows)
    section, span, contexts = plan.section, plan.span, plan.contexts
    half_head, half_units = HD // 2, units // 2
    half_push = half_head + half_units
    copies = micro_count * plan.shares
    score_scale = 1.0 / math.sqrt(HD)
    head_index = plan.tensor * heads_here + plan.head

    def in_order(own, other):
        return (jnp.where(section == 0, own, other), jnp.where(section == 0, other, own))

    def flat(place_section, place_context):
        return place_section * contexts + place_context

    def bring(origin, held):
        came = []
        for micro in range(micro_count):
            pairs = [
                (flat(origin, side * span + k), flat(side, micro * span + k))
                for side in range(micro_count)
                for k in range(span)
            ]
            came.append(lax.ppermute(held[micro], ("section", "context"), pairs))
        return jnp.where(plan.micro == 0, came[0], came[1])

    def take_home(own, target):
        came = []
        for micro in range(micro_count):
            pairs = [
                (flat(side, micro * span + k), flat(target, side * span + k))
                for side in range(micro_count)
                for k in range(span)
            ]
            came.append(lax.ppermute(own, ("section", "context"), pairs))
        return jnp.stack(came)

    def half_of(halves):
        kept = lax.dynamic_index_in_dim(halves, section, 0, keepdims=False)
        return kept, trade(lax.dynamic_index_in_dim(halves, 1 - section, 0, keepdims=False))

    def exchange(blocks):
        return lax.all_to_all(blocks, "context", split_axis=0, concat_axis=0, tiled=True)

    def repeat(half, layer):
        blocks = in_order(*half)[layer]
        spread = jnp.broadcast_to(blocks[None], (copies,) + blocks.shape)
        return spread.reshape((contexts,) + blocks.shape[1:])

    def split_qkv():
        blocks = qkv_weight[0].reshape(depth, 3, heads_here, 2, half_head)
        return half_of(blocks.transpose(3, 2, 0, 1, 4).reshape(2, heads_here, depth, 3 * half_head))

    def split_fc1():
        blocks = fc1_weight[0].reshape(depth, heads_here, 2, half_units)
        return half_of(blocks.transpose(2, 1, 0, 3))

    def split_push():
        blocks = jnp.concatenate(
            [
                out_weight[0].reshape(heads_here, 2, half_head, depth),
                fc2_weight[0].reshape(heads_here, 2, half_units, depth),
            ],
            axis=2,
        )
        return half_of(blocks.transpose(1, 0, 2, 3))

    def join_qkv(dealt):
        own = dealt.reshape(width, 3, half_head)
        low, high = in_order(own, trade(own))
        return jnp.stack([low, high], axis=2).reshape(width, 3 * HD)

    def join_fc1(dealt):
        own = dealt.reshape(width, half_units)
        return jnp.concatenate([own, trade(own)], axis=1)

    def join_push(dealt):
        own = dealt.transpose(1, 0, 2).reshape(half_push, width)
        return jnp.concatenate([own, trade(own)], axis=0)

    def gather_places():
        first = lax.all_gather(token_places[:, 0], "context", axis=0)
        return lax.dynamic_index_in_dim(first, plan.micro, 1, keepdims=False)

    def find_places(places):
        own_lengths = lax.dynamic_index_in_dim(lengths, plan.micro, 0, keepdims=False)
        own_spot = locate(plan.rows_of(places, section, plan.share), own_lengths)
        key_spots = [
            locate(plan.rows_of(places, section ^ side, plan.share ^ share), own_lengths)
            for side in range(2)
            for share in range(plan.shares)
        ]
        return own_spot, [jnp.concatenate(part) for part in zip(*key_spots)]

    def share_keys(value):
        held = [value]
        for share in range(1, plan.shares):
            held.append(flip(value, "context", share * heads_here))
        pile = jnp.concatenate(held, axis=0)
        return jnp.concatenate([pile, trade(pile)], axis=0)

    def return_keys(value):
        half = value.shape[0] // 2
        pile = value[:half] + trade(value[half:].astype(BF16)).astype(F32)
        total = pile[: plan.rows]
        for share in range(1, plan.shares):
            piece = pile[share * plan.rows : (share + 1) * plan.rows].astype(BF16)
            total = total + flip(piece, "context", share * heads_here).astype(F32)
        return total

    own_vector = jnp.concatenate(
        [
            norm_gain[0].reshape(-1),
            norm_bias[0].reshape(-1),
            branch_bias[0, 0] + branch_bias[0, 1],
            lax.dynamic_slice(qkv_bias[0], (0, head_index * HD), (3, HD)).reshape(-1),
            lax.dynamic_slice_in_dim(fc1_bias[0], head_index * units, units),
        ]
    )

    def unit_order(values):
        first, second = in_order(values[..., :half_units], values[..., half_units:])
        return jnp.concatenate([first, second], axis=-1)

    def cut_vector(vector):
        gain = vector[: 2 * width].reshape(2, width)
        bias = vector[2 * width : 4 * width].reshape(2, width)
        out_shift = vector[4 * width : 5 * width]
        qkv_shift = vector[5 * width : 5 * width + 3 * HD]
        return gain, bias, out_shift, qkv_shift, unit_order(vector[5 * width + 3 * HD :])

    def scaled_rows(full_rows):
        return normalize_parts(full_rows.astype(F32))[0]

    def norms(full_rows, vectors):
        gain, bias = vectors[:2]
        scaled = scaled_rows(full_rows)
        return [(scaled * gain[k] + bias[k]).astype(BF16) for k in range(2)]

    def project(norm_attn, qkv_full, vectors):
        projected = dot_nn(norm_attn, qkv_full) + vectors[3]
        queries = rotate_pairs(projected[:, :HD], cosine, sine_part).astype(BF16)
        key_rows = rotate_pairs(projected[:, HD : 2 * HD], cosine, sine_part).astype(BF16)
        value_rows = projected[:, 2 * HD :].astype(BF16)
        key_value = share_keys(jnp.concatenate([key_rows, value_rows], axis=1))
        return queries, key_value[:, :HD], key_value[:, HD:]

    def attend(queries, keys, values):
        scores = dot_nt(queries, keys) * score_scale
        masked = jnp.where(allowed, scores, MASKED)
        top = jnp.max(masked, axis=1, keepdims=True)
        weight = jnp.where(allowed, jnp.exp(masked - top), 0.0)
        probs = weight / jnp.sum(weight, axis=1, keepdims=True)
        return dot_nn(probs.astype(BF16), values).astype(BF16), probs

    def score_grads(values, probs, d_attended):
        d_probs = dot_nt(d_attended, values)
        centre = jnp.sum(probs * d_probs, axis=1, keepdims=True)
        return (probs * (d_probs - centre)).astype(BF16)

    def head_grads(queries, keys, probs, d_scores, d_attended):
        d_queries = dot_nn(d_scores, keys) * score_scale
        d_keys = dot_tn(d_scores, queries) * score_scale
        d_values = dot_tn(probs.astype(BF16), d_attended)
        return d_queries, jnp.concatenate([d_keys, d_values], axis=1)

    def turn_back(d_queries, d_key_values):
        key_grads = return_keys(d_key_values)
        return jnp.concatenate(
            [
                rotate_pairs(d_queries, cosine, -sine_part),
                rotate_pairs(key_grads[:, :HD], cosine, -sine_part),
                key_grads[:, HD:],
            ],
            axis=1,
        ).astype(BF16)

    def join_pushed(attended, hidden):
        first, second = in_order(attended[:, :half_head], attended[:, half_head:])
        return jnp.concatenate(
            [first, hidden[:, :half_units], second, hidden[:, half_units:]], axis=1
        )

    def cut_pushed(d_pushed):
        first, second = in_order(
            d_pushed[:, :half_head], d_pushed[:, half_push : half_push + half_head]
        )
        d_attended = jnp.concatenate([first, second], axis=1).astype(BF16)
        d_hidden = jnp.concatenate(
            [d_pushed[:, half_head:half_push], d_pushed[:, half_push + half_head :]], axis=1
        )
        return d_attended, d_hidden

    def push(pushed, push_full):
        return [dot_nn(rows, push_full).astype(BF16) for rows in plan.cut(pushed)]

    def add_branch(own_rows, summed, vectors):
        return (own_rows.astype(F32) + summed + vectors[2]).astype(BF16)

    def sum_cores(rows, own, other):
        came = trade(dot_tn(rows, other).astype(BF16))
        return (dot_tn(rows, own) + came.astype(F32)).astype(BF16)

    def push_blocks(pushed, grad_full):
        came = trade(dot_tn(pushed[:, half_push:], grad_full).astype(BF16))
        half = (dot_tn(pushed[:, :half_push], grad_full) + came.astype(F32)).astype(BF16)
        return half.reshape(half_push, contexts, depth).transpose(1, 0, 2)

    def fc1_blocks(norm_mlp, d_preact):
        half = sum_cores(norm_mlp, d_preact[:, :half_units], d_preact[:, half_units:])
        return half.reshape(contexts, depth, half_units)

    def qkv_blocks(norm_attn, d_projected):
        parts = d_projected.reshape(plan.rows, 3, 2, half_head)
        own, other = in_order(parts[:, :, 0], parts[:, :, 1])
        shape = (plan.rows, 3 * half_head)
        half = sum_cores(norm_attn, own.reshape(shape), other.reshape(shape))
        return half.reshape(contexts, depth, 3 * half_head)

    def gather_sum(came):
        return jnp.sum(came.reshape((copies, heads_here) + came.shape[1:]).astype(F32), axis=0)

    def norm_grads(d_projected, d_preact, qkv_full, fc1_full, full_rows, vectors, pin=None):
        d_norm_attn = dot_nt(d_projected, qkv_full)
        if pin is not None:
            d_norm_attn, d_preact = pin(d_norm_attn, d_preact)
        d_norm_mlp = dot_nt(d_preact, fc1_full)
        gain = vectors[0]
        d_scaled = (d_norm_attn * gain[0] + d_norm_mlp * gain[1]).astype(BF16)
        scaled = scaled_rows(full_rows)
        sums = [
            jnp.sum(d_norm_attn * scaled, axis=0),
            jnp.sum(d_norm_mlp * scaled, axis=0),
            jnp.sum(d_norm_attn, axis=0),
            jnp.sum(d_norm_mlp, axis=0),
        ]
        return d_scaled, sums

    def input_grad(grad_own, own_rows, d_scaled):
        own_scaled, own_inv = normalize_parts(own_rows.astype(F32))
        d_input = grad_own.astype(F32) + own_inv * (
            d_scaled
            - jnp.mean(d_scaled, axis=-1, keepdims=True)
            - own_scaled * jnp.mean(d_scaled * own_scaled, axis=-1, keepdims=True)
        )
        return d_input.astype(BF16)

    def vector_sums(norm_sums, d_projected, d_preact, grad_own):
        qkv_part = lax.dynamic_update_slice(
            jnp.zeros((3, width), F32),
            jnp.sum(d_projected, axis=0, dtype=F32).reshape(3, HD),
            (0, head_index * HD),
        )
        unit_part = lax.dynamic_update_slice_in_dim(
            jnp.zeros((all_units,), F32),
            unit_order(jnp.sum(d_preact, axis=0, dtype=F32)),
            head_index * units,
            0,
        )
        return jnp.concatenate(
            norm_sums
            + [jnp.sum(grad_own.astype(F32), axis=0), qkv_part.reshape(-1), unit_part]
        )

    def open_units(norm_mlp, fc1_full, vectors):
        preact = dot_nn(norm_mlp, fc1_full) + vectors[4]
        below = 0.5 * (1.0 + lax.erf(preact * math.sqrt(0.5)))
        bell = jnp.exp(-0.5 * preact * preact) * (1.0 / math.sqrt(2.0 * math.pi))
        return (preact * below).astype(BF16), below + preact * bell

    def finish(came0, came1):
        mine, yours = in_order(gather_sum(came0), gather_sum(came1))
        return jnp.stack(in_order(mine, trade(yours.astype(BF16)).astype(F32)))

    rows_in = [boundary[0, k] for k in range(micro_count)]
    first_rows = bring(0, rows_in)
    first_rows, qkv_weight, places, own_vector = pin(
        first_rows, qkv_weight, gather_places(), own_vector
    )
    qkv_half = split_qkv()

    def pin_gather(came):
        nonlocal qkv_half, own_vector, rows_in
        qkv_half, own_vector, rows_in, came = pin(qkv_half, own_vector, rows_in, came)
        return came

    full0 = plan.spread(first_rows, pins=[pin_gather])[0]
    qkv_in0 = repeat(qkv_half, 0)
    other_vector = trade(own_vector)
    grad1 = bring(1, rows_in)
    full0, qkv_in0, grad1, other_vector, fc1_weight, out_weight, fc2_weight = pin(
        full0, qkv_in0, grad1, other_vector, fc1_weight, out_weight, fc2_weight
    )
    (segment, position), (seg_keys, pos_keys) = find_places(places)
    fc1_half = split_fc1()
    fc1_in0 = repeat(fc1_half, 0)
    held1 = plan.pieces(grad1)
    vectors = [cut_vector(vector) for vector in in_order(own_vector, other_vector)]

    qkv_dealt0 = exchange(qkv_in0)
    norm_attn0, norm_mlp0 = norms(full0, vectors[0])
    push_half = split_push()
    qkv_dealt0, fc1_in0, push_half, norm_attn0, norm_mlp0, came1 = pin(
        qkv_dealt0, fc1_in0, push_half, norm_attn0, norm_mlp0, plan.send(held1, 0)
    )
    held1 = plan.join(held1, came1)
    fc1_dealt0 = exchange(fc1_in0)
    allowed = (segment[:, None] == seg_keys[None, :]) & (pos_keys[None, :] <= position[:, None])
    cosine, sine_part = angles(position)
    qkv0 = join_qkv(qkv_dealt0)
    queries0, keys0, values0 = project(norm_attn0, qkv0, vectors[0])
    push_in0 = repeat(push_half, 0)
    fc1_dealt0, push_in0, queries0, keys0, came1 = pin(
        fc1_dealt0, push_in0, queries0, keys0, plan.send(held1, 1)
    )
    held1 = plan.join(held1, came1)
    push_dealt0 = exchange(push_in0)
    attended0, probs0 = attend(queries0, keys0, values0)
    fc1_0 = join_fc1(fc1_dealt0)
    hidden0, slope0 = open_units(norm_mlp0, fc1_0, vectors[0])
    pushed0 = join_pushed(attended0, hidden0)
    qkv_in1, fc1_in1, push_in1 = [repeat(half, 1) for half in (qkv_half, fc1_half, push_half)]
    pushed0, probs0, slope0, push_dealt0, qkv_in1, fc1_in1, push_in1, came1 = pin(
        pushed0, probs0, slope0, push_dealt0, qkv_in1, fc1_in1, push_in1, plan.send(held1, 2)
    )
    grad_full1 = plan.whole(held1, came1)
    qkv_dealt1 = exchange(qkv_in1)
    push0 = join_push(push_dealt0)
    parts0 = push(pushed0, push0)

    def pin_deal(came):
        nonlocal qkv_dealt1
        qkv_dealt1, came = pin(qkv_dealt1, came)
        return came

    heads0 = plan.heads_of(full0)
    middle_rows, full1 = plan.sum_and_spread(
        parts0, lambda which, summed: add_branch(heads0[which], summed, vectors[0]), [pin_deal]
    )

    full1, qkv_dealt1, fc1_in1 = pin(full1, qkv_dealt1, fc1_in1)
    fc1_dealt1 = exchange(fc1_in1)
    qkv1 = join_qkv(qkv_dealt1)
    norm_attn1, norm_mlp1 = norms(full1, vectors[1])
    queries1, keys1, values1 = project(norm_attn1, qkv1, vectors[1])
    fc1_dealt1, push_in1, queries1, keys1 = pin(fc1_dealt1, push_in1, queries1, keys1)
    push_dealt1 = exchange(push_in1)
    attended1, probs1 = attend(queries1, keys1, values1)
    fc1_1 = join_fc1(fc1_dealt1)
    hidden1, slope1 = open_units(norm_mlp1, fc1_1, vectors[1])
    pushed1 = join_pushed(attended1, hidden1)
    push_back1 = push_blocks(pushed1, grad_full1)
    push_dealt1, push_back1, slope1, probs1 = pin(push_dealt1, push_back1, slope1, probs1)
    push_came1 = exchange(push_back1)
    push1 = join_push(push_dealt1)
    d_attended1, d_hidden1 = cut_pushed(dot_nt(grad_full1, push1))
    d_preact1 = (d_hidden1 * slope1).astype(BF16)
    fc1_back1 = fc1_blocks(norm_mlp1, d_preact1)
    d_scores1 = score_grads(values1, probs1, d_attended1)
    d_projected1 = turn_back(*head_grads(queries1, keys1, probs1, d_scores1, d_attended1))
    push_came1, fc1_back1, d_projected1 = pin(push_came1, fc1_back1, d_projected1)
    fc1_came1 = exchange(fc1_back1)
    d_scaled1, norm_sums1 = norm_grads(d_projected1, d_preact1, qkv1, fc1_1, full1, vectors[1])
    parts1 = plan.cut(d_scaled1)

    def pin_third(held):
        nonlocal fc1_came1
        fc1_came1, held = pin(fc1_came1, held)
        return held

    qkv_back1 = qkv_blocks(norm_attn1, d_projected1)
    last_parts = []

    def pin_push(came):
        nonlocal pushed1
        which = len(last_parts)
        part = dot_nn(plan.cut(pushed1)[which], push1).astype(BF16)
        part, pushed1, came = pin(part, pushed1, came)
        last_parts.append(part)
        return came

    grad_heads1, heads1 = plan.heads_of(grad_full1), plan.heads_of(full1)
    grad0, grad_full0 = plan.sum_and_spread(
        parts1,
        lambda which, summed: input_grad(grad_heads1[which], heads1[which], summed),
        [pin_third, pin_push, pin_push],
        [pin_push],
    )
    total1 = vector_sums(norm_sums1, d_projected1, d_preact1, grad1)

    grad_full0, qkv_back1, total1 = pin(grad_full0, qkv_back1, total1)
    qkv_came1 = exchange(qkv_back1)
    push_back0 = push_blocks(pushed0, grad_full0)
    push_back0, grad_full0, qkv_came1 = pin(push_back0, grad_full0, qkv_came1)
    push_came0 = exchange(push_back0)
    d_attended0, d_hidden0 = cut_pushed(dot_nt(grad_full0, push0))
    d_preact0 = (d_hidden0 * slope0).astype(BF16)
    fc1_back0 = fc1_blocks(norm_mlp0, d_preact0)
    d_scores0 = score_grads(values0, probs0, d_attended0)
    head_grads0 = head_grads(queries0, keys0, probs0, d_scores0, d_attended0)
    push_came0, fc1_back0, head_grads0, came = pin(
        push_came0, fc1_back0, head_grads0, plan.send_half(last_parts, 2)
    )
    fc1_came0 = exchange(fc1_back0)
    d_projected0 = turn_back(*head_grads0)
    d_projected0, last_parts, came = pin(d_projected0, last_parts, came)
    last_parts = plan.add_half(last_parts, came)
    qkv_back0 = qkv_blocks(norm_attn0, d_projected0)
    d_scaled0, norm_sums0 = norm_grads(d_projected0, d_preact0, qkv0, fc1_0, full0, vectors[0])
    fc1_came0, qkv_back0, d_scaled0, norm_sums0, push_came0, push_came1, came = pin(
        fc1_came0,
        qkv_back0,
        d_scaled0,
        norm_sums0,
        push_came0,
        push_came1,
        plan.send_half(last_parts, 1),
    )
    last_parts = plan.add_half(last_parts, came)
    total = jnp.stack([vector_sums(norm_sums0, d_projected0, d_preact0, grad0), total1])
    sums = [
        (axis, 1 << b)
        for axis in ("section", "context", "tensor")
        for b in range(int(math.log2(lax.axis_size(axis))))
    ]
    last_rows = last_home = None

    def pin_sum(came):
        nonlocal total, last_rows, last_home
        other = flip(total, *sums.pop(0))
        if last_rows is None:
            last_came, other, came = pin(plan.send_half(last_parts, 0), other, came)
            last_sum = [
                v[: v.shape[0] // 2].astype(F32) + w.astype(F32)
                for v, w in zip(last_parts, last_came)
            ]
            last_rows = add_branch(middle_rows, jnp.concatenate(last_sum, axis=0), vectors[1])
        elif last_home is None:
            last_home, other, came = pin(take_home(last_rows, 1), other, came)
        else:
            other, came = pin(other, came)
        total = total + other
        return came

    d_rows0 = plan.collect(plan.cut(d_scaled0), pins=[pin_sum] * len(plan.chunks))[0]
    d_input = input_grad(grad0, first_rows, d_rows0)
    qkv_back0, d_input, other, push_came0, push_came1, fc1_came0, fc1_came1 = pin(
        qkv_back0,
        d_input,
        flip(total, *sums.pop(0)),
        push_came0,
        push_came1,
        fc1_came0,
        fc1_came1,
    )
    total = total + other

    qkv_came0 = exchange(qkv_back0)
    first_home = take_home(d_input, 0)
    for spot in sums:
        total = total + flip(total, *spot)
    push_all = finish(push_came0, push_came1)
    fc1_all = finish(fc1_came0, fc1_came1)
    fc1_out = fc1_all.transpose(2, 1, 0, 3).reshape(depth, heads_here * units)
    out_out = push_all[:, :, :half_head].transpose(1, 0, 2, 3).reshape(heads_here * HD, depth)
    fc2_out = push_all[:, :, half_head:].transpose(1, 0, 2, 3).reshape(heads_here * units, depth)
    qkv_came0, last_home = pin(qkv_came0, last_home)
    result = jnp.where(section == 0, first_home, last_home)
    qkv_all = finish(qkv_came0, qkv_came1)
    qkv_out = (
        qkv_all.reshape(2, heads_here, depth, 3, half_head)
        .transpose(2, 3, 1, 0, 4)
        .reshape(depth, 3, heads_here * HD)
    )
    total = jnp.where(section == 0, total[0], total[1])
    return (
        result[None],
        qkv_out[None],
        out_out[None],
        fc1_out[None],
        fc2_out[None],
        total[: 2 * width].reshape(1, 2, width),
        total[2 * width : 4 * width].reshape(1, 2, width),
        total[5 * width : 8 * width].reshape(1, 3, width),
        total[8 * width :][None],
        jnp.broadcast_to(total[4 * width : 5 * width], (1, 2, width)),
    )


def solution(mesh):
    return jax.shard_map(
        per_device,
        mesh=mesh,
        in_specs=(
            P("section", None, ("context", "tensor"), None),
            P(None, "context"),
            P(),
            P("section", "context", None, "tensor"),
            P("section", "tensor", "context"),
            P("section", "context", "tensor"),
            P("section", "tensor", "context"),
            P("section", None, None),
            P("section", None, None),
            P("section", None, None),
            P("section", None),
            P("section", None, None),
        ),
        out_specs=(
            P("section", None, ("context", "tensor"), None),
            P("section", "context", None, "tensor"),
            P("section", "tensor", "context"),
            P("section", "context", "tensor"),
            P("section", "tensor", "context"),
            P("section", None, None),
            P("section", None, None),
            P("section", None, None),
            P("section", None),
            P("section", None, None),
        ),
        check_vma=False,
    )
```
